256 devices in a mesh: frame: 4 (over y_lo, core), patch: 64 (over y_hi, z, x).
Axes of the slice: x: 4, y: 4 (y_hi: 2, y_lo: 2; y = y_hi * 2 + y_lo), z: 8, core: 2. Of those that a mesh axis runs over, the one named last changes fastest.
Arguments:
- latent: bfloat16 [4, 64, 16, 1280], P(None, 'patch', None, 'frame'), may hold values from -24 to 24
- stale_latent: bfloat16 [4, 64, 16, 1280], P(None, 'patch', None, 'frame'), may hold values from -6 to 6
- conv_weight: bfloat16 [9, 1280, 1280], P(None, 'frame', 'patch'), may hold values from -1 to 1
- temb_table: bfloat16 [1000, 1280], replicated, may hold values from -4 to 4
- step_index: int32 [1], replicated, may hold values from 0 to 999
- gn_gain: float32 [1280], replicated, may hold values from 0.25 to 1.75
- gn_shift: float32 [1280], replicated, may hold values from -0.6 to 0.6
- w_sqkv: bfloat16 [1280, 3, 768], P('patch', None, 'frame'), may hold values from -0.15625 to 0.15625
- stale_kv: bfloat16 [4, 64, 16, 2, 768], P(None, 'patch', None, None, 'frame'), may hold values from -60 to 60
- w_sout: bfloat16 [768, 1280], P('frame', 'patch'), may hold values from -0.21875 to 0.21875
- w_tqkv: bfloat16 [1280, 3, 1280], P('patch', None, 'frame'), may hold values from -0.15625 to 0.15625
- w_tout: bfloat16 [1280, 1280], P('frame', 'patch'), may hold values from -0.15625 to 0.15625
Outputs:
- mixed: bfloat16 [4, 64, 16, 1280], P(None, 'patch')
- fresh_kv: bfloat16 [4, 64, 16, 2, 768], P(None, 'patch', None, None, 'frame')
The draws below stay inside these ranges and needn't reach their ends.
All inputs are finite; a program needn't handle non-finite values.
Results may differ from the reference program's by a relative error of at most 0.019.
Values may be sent and summed in bfloat16 or wider, within the bound.
No kernel may reach another device: no remote copies, remote signals or barrier semaphores. Data moves between devices by JAX's collectives and lax.ppermute only.
A program may use at most 128 MiB of HBM per device.

```python
import jax
import jax.numpy as jnp
from jax import lax

CHANNELS = 1280
GROUPS = 32
SHEADS = 12
THEADS = 20
HEAD_DIM = 64
FRAMES = 4
NUM_STEPS = 1000
BAND_ROWS = 1
COLUMNS = 16
FRAME_ROWS = 64
SPATIAL_INNER = 768


def draw_stale_kv(key, part):
    key = jax.random.fold_in(key, 11)
    first_key = jax.random.fold_in(key, 0)
    shape = (FRAMES, FRAME_ROWS, COLUMNS, 2, SHEADS * HEAD_DIM)
    values = jnp.clip(jax.random.normal(first_key, shape, jnp.float32), -6.0, 6.0)
    return values.astype(jnp.bfloat16)


def draw_latent(key, part):
    key = jax.random.fold_in(key, 23)
    shape = (FRAMES, FRAME_ROWS, COLUMNS, CHANNELS)
    position = (jnp.arange(FRAME_ROWS, dtype=jnp.float32) / max(FRAME_ROWS - 1, 1)).reshape(1, -1, 1, 1)
    noise = jnp.clip(jax.random.normal(key, shape, jnp.float32), -6.0, 6.0)
    scale = jnp.exp(jnp.log(3.0) * position)
    offset = 0.5 + 2.5 * position
    return (noise * scale + offset).astype(jnp.bfloat16)


def draw_conv_weight(key, part):
    key = jax.random.fold_in(key, 37)
    fan_in = 9.0 * CHANNELS
    noise = jnp.clip(jax.random.normal(key, (9, CHANNELS, CHANNELS), jnp.float32), -6.0, 6.0)
    return (noise / jnp.sqrt(fan_in) + 1.5 / fan_in).astype(jnp.bfloat16)


def levels(stream_key, dims, cuts, least, largest):
    def one(dim, blocks):
        steps = jax.random.uniform(jax.random.fold_in(jax.random.fold_in(stream_key, 6), dim), (blocks,), jnp.float32, least / len(cuts), largest / len(cuts))
        return jnp.repeat(jnp.exp(steps), dims[dim] // blocks).reshape((-1,) + (1,) * (len(dims) - dim - 1))

    factor_of = one(*cuts[0])
    for cut in cuts[1:]:
        factor_of = factor_of * one(*cut)
    return factor_of


def gaussian(own_key, shape, spread, bound, pieces=(), kind=jnp.bfloat16):
    factor_of = levels(own_key, shape, pieces, -0.22, 0.18) if pieces else 1.0
    array = jax.random.normal(own_key, shape, jnp.float32) * spread * factor_of
    return jnp.minimum(jnp.maximum(array, -bound), bound).astype(kind)


def setup_inputs(seed: int = 0) -> dict:
    key_of = jax.random.split(jax.random.key(seed), 13)
    return {
        "latent": draw_latent(jax.random.fold_in(key_of[12], 71), 0),
        "stale_latent": gaussian(key_of[1], (FRAMES, FRAME_ROWS, COLUMNS, CHANNELS), 1.0, 6.0, ((1, 64), (3, 4))),
        "conv_weight": draw_conv_weight(jax.random.fold_in(key_of[12], 71), 0),
        "temb_table": gaussian(key_of[3], (NUM_STEPS, CHANNELS), 0.6, 4.0),
        "step_index": jax.random.randint(key_of[4], (1,), 0, NUM_STEPS).astype(jnp.int32),
        "gn_gain": jnp.clip(1.0 + 0.15 * jax.random.normal(key_of[5], (CHANNELS,), jnp.float32), 0.25, 1.75),
        "gn_shift": jnp.clip(jax.random.uniform(key_of[6], (CHANNELS,), jnp.float32, -0.6, 0.6), -0.6, 0.6),
        "w_sqkv": gaussian(key_of[7], (CHANNELS, 3, SPATIAL_INNER), CHANNELS ** -0.5, 0.15625, ((0, 64), (2, 4))),
        "stale_kv": draw_stale_kv(jax.random.fold_in(key_of[12], 71), 0),
        "w_sout": gaussian(key_of[9], (SPATIAL_INNER, CHANNELS), SPATIAL_INNER ** -0.5, 0.21875, ((0, 4), (1, 64))),
        "w_tqkv": gaussian(key_of[10], (CHANNELS, 3, CHANNELS), CHANNELS ** -0.5, 0.15625, ((0, 64), (2, 4))),
        "w_tout": gaussian(key_of[11], (CHANNELS, CHANNELS), CHANNELS ** -0.5, 0.15625, ((0, 4), (1, 64))),
    }


def conv_rows(latent, stale_latent):
    rows = jnp.arange(FRAME_ROWS, dtype=jnp.int32).reshape(1, -1, 1, 1)
    zero_row = jnp.zeros_like(latent[:, :1])
    above_fresh = jnp.concatenate([zero_row, latent[:, :-1]], axis=1)
    above_stale = jnp.concatenate([zero_row, stale_latent[:, :-1]], axis=1)
    below_fresh = jnp.concatenate([latent[:, 1:], zero_row], axis=1)
    below_stale = jnp.concatenate([stale_latent[:, 1:], zero_row], axis=1)
    above = jnp.where(rows % BAND_ROWS == 0, above_stale, above_fresh)
    below = jnp.where(rows % BAND_ROWS == BAND_ROWS - 1, below_stale, below_fresh)
    return [above, latent, below]

def reference(latent, stale_latent, conv_weight, temb_table, step_index, gn_gain, gn_shift, w_sqkv, stale_kv, w_sout, w_tqkv, w_tout):
    sources = conv_rows(latent, stale_latent)
    hidden = jnp.zeros((FRAMES * FRAME_ROWS * COLUMNS, CHANNELS), jnp.float32)
    for row_tap in range(3):
        padded = jnp.pad(sources[row_tap], ((0, 0), (0, 0), (1, 1), (0, 0)))
        for col_tap in range(3):
            window = padded[:, :, col_tap:col_tap + COLUMNS].reshape(-1, CHANNELS)
            hidden = hidden + jnp.dot(window, conv_weight[3 * row_tap + col_tap], preferred_element_type=jnp.float32)
    embed = lax.dynamic_slice_in_dim(temb_table, step_index[0], 1, 0).astype(jnp.float32)
    hidden = hidden + embed
    grouped = hidden.reshape(FRAMES, FRAME_ROWS * COLUMNS, GROUPS, CHANNELS // GROUPS)
    mean = lax.optimization_barrier(jnp.mean(grouped, axis=(1, 3), keepdims=True))
    centred = grouped - mean
    variance = lax.optimization_barrier(jnp.mean(centred * centred, axis=(1, 3), keepdims=True))
    normed = (centred * lax.rsqrt(variance + 1e-05)).reshape(FRAMES, FRAME_ROWS, COLUMNS, CHANNELS)
    activated = jax.nn.silu(normed * gn_gain + gn_shift).astype(jnp.bfloat16)
    projected = jnp.dot(activated.reshape(-1, CHANNELS), w_sqkv.reshape(CHANNELS, -1), preferred_element_type=jnp.float32)
    projected = projected.astype(jnp.bfloat16).reshape(FRAMES, FRAME_ROWS, COLUMNS, 3, SPATIAL_INNER)
    fresh_kv = projected[:, :, :, 1:]
    queries = projected[:, :, :, 0]
    score_scale = HEAD_DIM ** (-0.5)
    row_band = (jnp.arange(FRAME_ROWS, dtype=jnp.int32) // BAND_ROWS).reshape(1, -1, 1, 1, 1)

    def one_band(band_index):
        band_queries = lax.dynamic_slice_in_dim(queries, band_index * BAND_ROWS, BAND_ROWS, 1)
        band_queries = band_queries.reshape(FRAMES, BAND_ROWS * COLUMNS, SHEADS, HEAD_DIM).astype(jnp.float32)
        chosen = jnp.where(row_band == band_index, fresh_kv, stale_kv)
        keys = chosen[:, :, :, 0].reshape(FRAMES, FRAME_ROWS * COLUMNS, SHEADS, HEAD_DIM).astype(jnp.float32)
        values = chosen[:, :, :, 1].reshape(FRAMES, FRAME_ROWS * COLUMNS, SHEADS, HEAD_DIM).astype(jnp.float32)
        scores = jnp.einsum('fqhd,fkhd->fhqk', band_queries, keys) * score_scale
        expo = jnp.exp(scores - lax.optimization_barrier(jnp.max(scores, axis=-1, keepdims=True)))
        denominator = lax.optimization_barrier(jnp.sum(expo, axis=-1))
        weights = expo.astype(jnp.bfloat16).astype(jnp.float32)
        numerator = jnp.einsum('fhqk,fkhd->fhqd', weights, values)
        result = (numerator / denominator[..., None]).astype(jnp.bfloat16)
        return jnp.transpose(result, (0, 2, 1, 3)).reshape(FRAMES, BAND_ROWS, COLUMNS, SPATIAL_INNER)
    band_outputs = lax.map(one_band, jnp.arange(FRAME_ROWS // BAND_ROWS, dtype=jnp.int32))
    spatial_out = jnp.transpose(band_outputs, (1, 0, 2, 3, 4)).reshape(-1, SPATIAL_INNER)
    spatial_sum = jnp.dot(spatial_out, w_sout, preferred_element_type=jnp.float32)
    section = (activated.reshape(-1, CHANNELS).astype(jnp.float32) + spatial_sum).astype(jnp.bfloat16)
    temporal = jnp.dot(section, w_tqkv.reshape(CHANNELS, -1), preferred_element_type=jnp.float32).astype(jnp.bfloat16)
    temporal = temporal.reshape(FRAMES, FRAME_ROWS * COLUMNS, 3, THEADS, HEAD_DIM).astype(jnp.float32)
    scores = jnp.einsum('fthd,gthd->thfg', temporal[:, :, 0], temporal[:, :, 1]) * score_scale
    expo = jnp.exp(scores - lax.optimization_barrier(jnp.max(scores, axis=-1, keepdims=True)))
    denominator = lax.optimization_barrier(jnp.sum(expo, axis=-1))
    weights = expo.astype(jnp.bfloat16).astype(jnp.float32)
    numerator = jnp.einsum('thfg,gthd->fthd', weights, temporal[:, :, 2])
    temporal_out = (numerator / jnp.transpose(denominator, (2, 0, 1))[..., None]).astype(jnp.bfloat16)
    temporal_sum = jnp.dot(temporal_out.reshape(-1, CHANNELS), w_tout, preferred_element_type=jnp.float32)
    mixed = (section.astype(jnp.float32) + temporal_sum).astype(jnp.bfloat16)
    return (mixed.reshape(FRAMES, FRAME_ROWS, COLUMNS, CHANNELS), fresh_kv)
```

```python
import jax
import jax.numpy as jnp
from jax import lax
from jax.experimental import pallas as pl
from jax.experimental.pallas import tpu as pltpu
from jax.sharding import Mesh
from jax.sharding import PartitionSpec as P

CHANNELS = 1280
GROUPS = 32
GROUP_WIDTH = CHANNELS // GROUPS
HEAD_DIM = 64
FRAMES = 4
COLUMNS = 16
SIZES = {"yl": 2, "c": 2, "yh": 2, "z": 8, "x": 4}
FRAME = ("yl", "c")
PATCH = ("yh", "z", "x")
RING = (0, 1, 7, 2, 6, 3, 5, 4)
BF16 = jnp.bfloat16
F32 = jnp.float32
VMEM = pl.BlockSpec(memory_space=pltpu.VMEM)
SMEM = pl.BlockSpec(memory_space=pltpu.SMEM)
PARAMS = pltpu.CompilerParams(vmem_limit_bytes=40 * 1024 * 1024)
NT = (((1,), (1,)), ((), ()))


def from_shift(value, axis, offset):
    size = SIZES[axis]
    return lax.ppermute(value, axis, [((i + offset) % size, i) for i in range(size)])


def ring_gather(block):
    ahead, behind = [block], [block]
    for _ in range(3):
        ahead.append(from_shift(ahead[-1], "z", 1))
        behind.append(from_shift(behind[-1], "z", -1))
    far = from_shift(ahead[-1], "z", 1)
    return [block, ahead[1], behind[1], ahead[2], behind[2], ahead[3], behind[3], far]


def gather_yx(block, yh, x):
    other = from_shift(block, "yh", 1)
    pair = jnp.stack([jnp.where(yh == 0, block, other), jnp.where(yh == 0, other, block)])
    parts = [pair] + [from_shift(pair, "x", k) for k in (1, 2, 3)]
    ordered = []
    for place in range(4):
        chosen = parts[place]
        for mine in (1, 2, 3):
            chosen = jnp.where(x == mine, parts[(place - mine) % 4], chosen)
        ordered.append(chosen)
    return jnp.concatenate(ordered, axis=1).reshape(160, -1)


def conv_kernel(where_ref, rows_ref, weight_ref, keep_ref, send_ref):
    yl, c = where_ref[0], where_ref[1]
    column = lax.broadcasted_iota(jnp.int32, (512, 1), 0) % COLUMNS
    sums = []
    for col_tap in range(3):
        total = None
        for row_tap in range(3):
            lhs = rows_ref[:, row_tap].reshape(512, 320)
            tap = 3 * row_tap + col_tap
            part = lax.dot_general(
                lhs,
                weight_ref[:, tap * 320 : (tap + 1) * 320],
                NT,
                preferred_element_type=F32,
            )
            total = part if total is None else total + part
        sums.append(total)
    left = jnp.where(column == 0, 0.0, pltpu.roll(sums[0], 1, 0))
    right = jnp.where(column == COLUMNS - 1, 0.0, pltpu.roll(sums[2], 511, 0))
    hidden = (sums[1] + left + right).reshape(8, FRAMES, COLUMNS, 160)
    for frame in range(FRAMES):
        value = hidden[:, frame].reshape(128, 160)
        place = yl ^ (frame // 2)

        @pl.when(c == frame % 2)
        def _():
            keep_ref[place] = value

        @pl.when(c != frame % 2)
        def _():
            send_ref[place] = value


def group_masks():
    lane = lax.broadcasted_iota(jnp.int32, (1, 160), 1)
    return [(lane // GROUP_WIDTH) == g for g in range(4)]


def stats_kernel(keep_ref, got_ref, embed_ref, hidden_ref, stats_ref):
    hidden = keep_ref[...] + got_ref[...] + embed_ref[...]
    hidden_ref[...] = hidden
    count = 128.0 * GROUP_WIDTH
    masks = group_masks()
    sums = jnp.sum(hidden, axis=0, keepdims=True)
    means = [jnp.sum(jnp.where(m, sums, 0.0), axis=1, keepdims=True) / count for m in masks]
    mean = sum(jnp.where(m, v, 0.0) for m, v in zip(masks, means))
    centred = hidden - mean
    squares = jnp.sum(centred * centred, axis=0, keepdims=True)
    lane = lax.broadcasted_iota(jnp.int32, (8, 128), 1)
    out = jnp.zeros((8, 128), F32)
    for g in range(4):
        spread = jnp.sum(jnp.where(masks[g], squares, 0.0), axis=1, keepdims=True)
        out = jnp.where(lane == g, means[g], out)
        out = jnp.where(lane == 4 + g, spread, out)
    stats_ref[...] = out


def norm_kernel(hidden_ref, stats_ref, gain_ref, shift_ref, out_ref):
    stats = stats_ref[...]
    masks = group_masks()
    local = 128.0 * GROUP_WIDTH
    mean_row = jnp.zeros((1, 160), F32)
    scale_row = jnp.zeros((1, 160), F32)
    for g in range(4):
        means = stats[:, 0:1, g : g + 1]
        mean = jnp.sum(means, axis=0, keepdims=True) / 8.0
        gap = means - mean
        spread = jnp.sum(stats[:, 0:1, 4 + g : 5 + g] + local * gap * gap, axis=0) / (8.0 * local)
        mean_row = jnp.where(masks[g], mean[0], mean_row)
        scale_row = jnp.where(masks[g], lax.rsqrt(spread + 1e-05), scale_row)
    normed = (hidden_ref[...] - mean_row) * scale_row
    value = normed * gain_ref[...] + shift_ref[...]
    out_ref[...] = jax.nn.silu(value).astype(BF16).reshape(8, COLUMNS, 160)


def softmax_parts(scores):
    top = jnp.max(scores, axis=-1, keepdims=True)
    expo = jnp.exp(scores - top)
    return expo.astype(BF16), jnp.sum(expo, axis=-1, keepdims=True)


def spatial_kernel(where_ref, *refs):
    acts, weights, stale = refs[:4], refs[4:12], refs[12:16]
    keep_ref, send_ref, fresh_ref, own_ref, w_scr = refs[16:]
    yl, c, z = where_ref[0], where_ref[1], where_ref[2]
    for ref, offset in zip(weights, RING):
        w_scr[(z + offset) % 8] = ref[...]
    projected = None
    for chunk in range(8):
        lhs = jnp.concatenate([a[chunk] for a in acts], axis=0)
        part = jnp.dot(lhs, w_scr[chunk, :, :576], preferred_element_type=F32)
        projected = part if projected is None else projected + part
    projected = projected.astype(BF16)
    own_ref[...] = jnp.concatenate([acts[0][chunk] for chunk in range(8)], axis=1)
    score_scale = HEAD_DIM ** (-0.5)
    attended = []
    for rel in range(FRAMES):
        frame = (2 * yl + c) ^ rel
        mine = projected[rel * COLUMNS : (rel + 1) * COLUMNS]
        fresh_ref[frame] = mine[:, 192:]
        blocks = [r[:, frame].reshape(256, 384) for r in stale]
        blocks[0] = jnp.concatenate([mine[:, 192:], blocks[0][COLUMNS:]], axis=0)
        query = mine[:, :192]
        head_of = lax.broadcasted_iota(jnp.int32, (COLUMNS, 192), 1) // HEAD_DIM
        zero = jnp.zeros_like(query)
        queries = jnp.concatenate([jnp.where(head_of == h, query, zero) for h in range(3)], axis=0)
        scores = jnp.concatenate(
            [
                lax.dot_general(queries, b[:, :192], NT, preferred_element_type=F32)
                for b in blocks
            ],
            axis=1,
        )
        expo, total = softmax_parts(scores * score_scale)
        numerator = None
        for i, b in enumerate(blocks):
            part = jnp.dot(
                expo[:, i * 256 : (i + 1) * 256], b[:, 192:], preferred_element_type=F32
            )
            numerator = part if numerator is None else numerator + part
        result = numerator / total
        rows = jnp.zeros((COLUMNS, 192), F32)
        for h in range(3):
            rows = jnp.where(head_of == h, result[h * COLUMNS : (h + 1) * COLUMNS], rows)
        attended.append(rows.astype(BF16))
    attended = jnp.concatenate(attended, axis=0)
    for chunk in range(8):
        part = lax.dot_general(
            attended, w_scr[chunk, :, 576:768], NT, preferred_element_type=F32
        )
        lanes = slice(chunk * 160, (chunk + 1) * 160)
        for rel in range(FRAMES):
            target = send_ref if rel % 2 else keep_ref
            target[rel // 2, :, lanes] = part[rel * COLUMNS : (rel + 1) * COLUMNS]


def temporal_kernel(where_ref, *refs):
    pieces, weights = refs[:4], refs[4:12]
    keep_ref, send_ref, w_scr, out_scr = refs[12:]
    z = where_ref[2]
    for ref, offset in zip(weights, RING):
        chunk = (z + offset) % 8
        w_scr[chunk] = ref[:, :960]
        for half in range(2):
            out_scr[half, chunk] = ref[half * 80 : (half + 1) * 80, 960:]
    section = jnp.concatenate([p[...] for p in pieces], axis=0)
    temporal = None
    for chunk in range(8):
        part = jnp.dot(
            section[:, chunk * 160 : (chunk + 1) * 160], w_scr[chunk], preferred_element_type=F32
        )
        temporal = part if temporal is None else temporal + part
    temporal = temporal.astype(BF16)
    score_scale = HEAD_DIM ** (-0.5)
    row = lax.broadcasted_iota(jnp.int32, (64, 64), 0) % COLUMNS
    col = lax.broadcasted_iota(jnp.int32, (64, 64), 1) % COLUMNS
    outs = []
    for head in range(5):
        query, key, value = [
            temporal[:, k * 320 + head * 64 : k * 320 + (head + 1) * 64] for k in range(3)
        ]
        scores = lax.dot_general(query, key, NT, preferred_element_type=F32) * score_scale
        expo, total = softmax_parts(jnp.where(row == col, scores, -jnp.inf))
        outs.append(jnp.dot(expo, value, preferred_element_type=F32) / total)
    mixed = jnp.concatenate(outs, axis=1).astype(BF16)
    part = lax.dot_general(
        mixed, out_scr[...].reshape(CHANNELS, 320), NT, preferred_element_type=F32
    )
    for rel in range(FRAMES):
        target = send_ref if rel % 2 else keep_ref
        target[rel // 2] = part[rel * COLUMNS : (rel + 1) * COLUMNS]


def final_kernel(where_ref, *refs):
    out_ref = refs[4]
    mine = 2 * where_ref[0] + where_ref[1]
    for rel in range(FRAMES):
        out_ref[mine ^ rel] = refs[rel][...]


def call(kernel, out_shape, *args, scratch=(), flops=0, smem=False):
    moved = sum(a.size * a.dtype.itemsize for a in args)
    return pl.pallas_call(
        kernel,
        out_shape=out_shape,
        in_specs=[SMEM if smem and i == 0 else VMEM for i in range(len(args))],
        out_specs=jax.tree.map(lambda _: VMEM, out_shape),
        scratch_shapes=list(scratch),
        compiler_params=PARAMS,
        cost_estimate=pl.CostEstimate(flops=flops, bytes_accessed=moved, transcendentals=0),
    )(*args)


def shape(dims, dtype):
    return jax.ShapeDtypeStruct(dims, dtype)


def swap(value, axis):
    return lax.ppermute(value, axis, [(0, 1), (1, 0)])


def sum_over_frame(keep, send):
    got = swap(send, "c")
    away = keep[1] + got[1]
    return keep[0] + got[0], swap(away, "yl")


def gather_frame(piece):
    other = swap(piece, "c")
    return [piece, other, swap(piece, "yl"), swap(other, "yl")]


def shards(
    latent,
    stale_latent,
    conv_weight,
    temb_table,
    step_index,
    gn_gain,
    gn_shift,
    w_sqkv,
    stale_kv,
    w_sout,
    w_tqkv,
    w_tout,
):
    yl, c, yh, z, x = (lax.axis_index(a) for a in ("yl", "c", "yh", "z", "x"))
    where = jnp.stack([yl, c, z, yh, x]).astype(jnp.int32)

    count = 64
    above = lax.ppermute(stale_latent, PATCH, [(i, i + 1) for i in range(count - 1)])
    below = lax.ppermute(stale_latent, PATCH, [(i + 1, i) for i in range(count - 1)])
    conv_block = jnp.transpose(conv_weight, (2, 0, 1)).reshape(20, 9 * 320)
    conv_full = gather_yx(conv_block, yh, x)

    small = jnp.concatenate(
        [w_sqkv.reshape(20, 576), w_sout.T, w_tqkv.reshape(20, 960), w_tout.T], axis=1
    )
    block = gather_yx(small, yh, x)
    first = ring_gather(block[:, :768])
    second = ring_gather(block[:, 768:])

    kv = stale_kv.reshape(FRAMES, COLUMNS, 384)
    kv_pair = jnp.stack([kv, from_shift(kv, "yh", 1)])
    kv_rows = jnp.concatenate(ring_gather(kv_pair), axis=0)
    kv_blocks = [kv_rows] + [from_shift(kv_rows, "x", k) for k in (1, 3, 2)]

    rows = jnp.concatenate([above, latent, below], axis=1).transpose(1, 0, 2, 3)
    rows = lax.all_to_all(jnp.broadcast_to(rows, (8,) + rows.shape), "z", 0, 0)
    half = shape((2, 128, 160), F32)
    keep, send = call(conv_kernel, (half, half), where, rows, conv_full, smem=True, flops=3 * 10**9)
    mine, got = sum_over_frame(keep, send)

    def channels_of(vector):
        return lax.dynamic_index_in_dim(vector.reshape(2, 8, 80), z, 1, keepdims=False).reshape(1, 160)

    embed = channels_of(lax.dynamic_index_in_dim(temb_table, step_index[0], 0, keepdims=False))
    hidden, stats = call(
        stats_kernel, (shape((128, 160), F32), shape((8, 128), F32)), mine, got, embed.astype(F32)
    )
    stats = lax.all_to_all(jnp.broadcast_to(stats, (8, 8, 128)), ("yh", "x"), 0, 0)
    activated = call(
        norm_kernel,
        shape((8, COLUMNS, 160), BF16),
        hidden,
        stats,
        channels_of(gn_gain),
        channels_of(gn_shift),
    )
    activated = lax.all_to_all(activated, "z", 0, 0)

    share = shape((2, COLUMNS, CHANNELS), F32)
    keep, send, fresh, own = call(
        spatial_kernel,
        (share, share, shape((FRAMES, COLUMNS, 384), BF16), shape((COLUMNS, CHANNELS), BF16)),
        where,
        *gather_frame(activated),
        *first,
        *kv_blocks,
        smem=True,
        scratch=[pltpu.VMEM((8, 160, 768), BF16)],
        flops=10**9,
    )
    mine, got = sum_over_frame(keep, send)
    section = (own.astype(F32) + (mine + got)).astype(BF16)
    keep, send = call(
        temporal_kernel,
        (share, share),
        where,
        *gather_frame(section),
        *second,
        smem=True,
        scratch=[pltpu.VMEM((8, 160, 960), BF16), pltpu.VMEM((2, 8, 80, 320), BF16)],
        flops=10**9,
    )
    mine, got = sum_over_frame(keep, send)
    mixed = (section_standard(section).astype(F32) + (mine + got)).astype(BF16)
    mixed = call(
        final_kernel,
        shape((FRAMES, COLUMNS, CHANNELS), BF16),
        where,
        *gather_frame(mixed),
        smem=True,
    )
    return (
        mixed.reshape(FRAMES, 1, COLUMNS, CHANNELS),
        fresh.reshape(FRAMES, 1, COLUMNS, 2, 192),
    )


def section_standard(section):
    return section.reshape(COLUMNS, 8, 2, 80).transpose(0, 2, 1, 3).reshape(COLUMNS, CHANNELS)


def solution(mesh):
    fine = Mesh(mesh.devices.reshape(2, 2, 2, 8, 4), ("yl", "c", "yh", "z", "x"))
    return jax.shard_map(
        shards,
        mesh=fine,
        in_specs=(
            P(None, PATCH, None, FRAME),
            P(None, PATCH, None, FRAME),
            P(None, FRAME, PATCH),
            P(),
            P(),
            P(),
            P(),
            P(PATCH, None, FRAME),
            P(None, PATCH, None, None, FRAME),
            P(FRAME, PATCH),
            P(PATCH, None, FRAME),
            P(FRAME, PATCH),
        ),
        out_specs=(P(None, PATCH, None, None), P(None, PATCH, None, None, FRAME)),
        check_vma=False,
    )
```

```python
import jax
import jax.numpy as jnp
from jax import lax
from jax.experimental import pallas as pl
from jax.experimental.pallas import tpu as pltpu
from jax.sharding import Mesh
from jax.sharding import PartitionSpec as P

CHANNELS = 1280
GROUPS = 32
GROUP_WIDTH = CHANNELS // GROUPS
HEAD_DIM = 64
FRAMES = 4
COLUMNS = 16
SIZES = {"yl": 2, "c": 2, "yh": 2, "z": 8, "x": 4}
FRAME = ("yl", "c")
PATCH = ("yh", "z", "x")
BF16 = jnp.bfloat16
F32 = jnp.float32
VMEM = pl.BlockSpec(memory_space=pltpu.VMEM)
SMEM = pl.BlockSpec(memory_space=pltpu.SMEM)
HBM = pl.BlockSpec(memory_space=pl.ANY)
PARAMS = pltpu.CompilerParams(vmem_limit_bytes=40 * 1024 * 1024)
NT = (((1,), (1,)), ((), ()))


def from_shift(value, axis, offset):
    size = SIZES[axis]
    return lax.ppermute(value, axis, [((i + offset) % size, i) for i in range(size)])


def pair_yh(block, yh):
    other = from_shift(block, "yh", 1)
    return jnp.concatenate(
        [jnp.where(yh == 0, block, other), jnp.where(yh == 0, other, block)], axis=0
    )


def gather_x(pair, x):
    parts = [pair] + [from_shift(pair, "x", k) for k in (1, 2, 3)]
    ordered = []
    for place in range(4):
        chosen = parts[place]
        for mine in (1, 2, 3):
            chosen = jnp.where(x == mine, parts[(place - mine) % 4], chosen)
        ordered.append(chosen)
    return ordered


def conv_kernel(where_ref, rows_ref, weight_ref, keep_ref, send_ref):
    yl, c = where_ref[0], where_ref[1]
    column = lax.broadcasted_iota(jnp.int32, (512, 1), 0) % COLUMNS
    sums = []
    for col_tap in range(3):
        total = None
        for row_tap in range(3):
            lhs = rows_ref[:, row_tap].reshape(512, 320)
            tap = 3 * row_tap + col_tap
            part = lax.dot_general(
                lhs,
                weight_ref[:, tap * 320 : (tap + 1) * 320],
                NT,
                preferred_element_type=F32,
            )
            total = part if total is None else total + part
        sums.append(total)
    left = jnp.where(column == 0, 0.0, pltpu.roll(sums[0], 1, 0))
    right = jnp.where(column == COLUMNS - 1, 0.0, pltpu.roll(sums[2], 511, 0))
    hidden = (sums[1] + left + right).reshape(8, FRAMES, COLUMNS, 160)
    for frame in range(FRAMES):
        value = hidden[:, frame].reshape(128, 160)
        place = yl ^ (frame // 2)

        @pl.when(c == frame % 2)
        def _():
            keep_ref[place] = value

        @pl.when(c != frame % 2)
        def _():
            send_ref[place] = value


def group_masks():
    lane = lax.broadcasted_iota(jnp.int32, (1, 160), 1)
    return [(lane // 80) * 2 + (lane % 40) // 20 == g for g in range(4)]


def stats_kernel(keep_ref, got_ref, embed_ref, hidden_ref, stats_ref):
    hidden = keep_ref[...] + got_ref[...] + embed_ref[...]
    hidden_ref[...] = hidden
    count = 128.0 * GROUP_WIDTH
    masks = group_masks()
    sums = jnp.sum(hidden, axis=0, keepdims=True)
    means = [jnp.sum(jnp.where(m, sums, 0.0), axis=1, keepdims=True) / count for m in masks]
    mean = sum(jnp.where(m, v, 0.0) for m, v in zip(masks, means))
    centred = hidden - mean
    squares = jnp.sum(centred * centred, axis=0, keepdims=True)
    lane = lax.broadcasted_iota(jnp.int32, (8, 128), 1)
    out = jnp.zeros((8, 128), F32)
    for g in range(4):
        spread = jnp.sum(jnp.where(masks[g], squares, 0.0), axis=1, keepdims=True)
        out = jnp.where(lane == g, means[g], out)
        out = jnp.where(lane == 4 + g, spread, out)
    stats_ref[...] = out


def norm_kernel(hidden_ref, stats_ref, gain_ref, shift_ref, out_ref):
    stats = stats_ref[...]
    masks = group_masks()
    local = 128.0 * GROUP_WIDTH
    mean_row = jnp.zeros((1, 160), F32)
    scale_row = jnp.zeros((1, 160), F32)
    for g in range(4):
        means = stats[:, 0:1, g : g + 1]
        mean = jnp.sum(means, axis=0, keepdims=True) / 8.0
        gap = means - mean
        spread = jnp.sum(stats[:, 0:1, 4 + g : 5 + g] + local * gap * gap, axis=0) / (8.0 * local)
        mean_row = jnp.where(masks[g], mean[0], mean_row)
        scale_row = jnp.where(masks[g], lax.rsqrt(spread + 1e-05), scale_row)
    normed = (hidden_ref[...] - mean_row) * scale_row
    value = normed * gain_ref[...] + shift_ref[...]
    out_ref[...] = jax.nn.silu(value).astype(BF16).reshape(8, COLUMNS, 160)


def softmax_parts(scores):
    top = jnp.max(scores, axis=-1, keepdims=True)
    expo = jnp.exp(scores - top)
    return expo.astype(BF16), jnp.sum(expo, axis=-1, keepdims=True)


def order_matrix():
    row = lax.broadcasted_iota(jnp.int32, (160, 160), 0)
    col = lax.broadcasted_iota(jnp.int32, (160, 160), 1)
    return (row // 40 * 20 + row % 20 + (row % 40) // 20 * 80 == col).astype(BF16)


def reorder_rows(turn, chunks):
    turned = []
    for rows in chunks:
        value = lax.dot_general(turn, rows, (((0,), (0,)), ((), ())), preferred_element_type=F32)
        turned.append(value.astype(BF16))
    return jnp.concatenate([t[80 * h : 80 * h + 80] for h in range(2) for t in turned], axis=0)


def chunk_of(w_scr, chunk, blocks):
    places = slice(4 * chunk, 4 * chunk + 4)
    parts = [w_scr[places, 40 * k : 40 * k + 40, :].reshape(160, 384) for k in blocks]
    return jnp.concatenate(parts, axis=1)


def spatial_kernel(where_ref, *refs):
    acts, packed_ref = refs[:4], refs[4]
    keep_ref, send_ref, fresh_ref, own_ref, w_scr, kv_scr, w_sem, kv_sem = refs[5:]
    w_copy = pltpu.make_async_copy(packed_ref.at[:, 128:208], w_scr, w_sem)
    kv_copy = pltpu.make_async_copy(packed_ref.at[:, :128], kv_scr, kv_sem)
    w_copy.start()
    kv_copy.start()
    yl, c, place = where_ref[0], where_ref[1], where_ref[2] * 4 + where_ref[4]
    turn = order_matrix()
    own = [
        jnp.dot(acts[0][chunk], turn, preferred_element_type=F32).astype(BF16) for chunk in range(8)
    ]
    own_ref[...] = jnp.concatenate([o[:, 80 * h : 80 * h + 80] for h in range(2) for o in own], axis=1)
    w_copy.wait()
    projected = None
    out_weights = []
    for chunk in range(8):
        lhs = jnp.concatenate([a[chunk] for a in acts], axis=0)
        rhs = chunk_of(w_scr, chunk, (0, 1))
        part = jnp.dot(lhs, rhs[:, :576], preferred_element_type=F32)
        projected = part if projected is None else projected + part
        out_weights.append(rhs[:, 576:])
    projected = projected.astype(BF16)
    out_weights = reorder_rows(turn, out_weights)
    score_scale = HEAD_DIM ** (-0.5)
    head_of = lax.broadcasted_iota(jnp.int32, (COLUMNS, 192), 1) // HEAD_DIM
    key_row = lax.broadcasted_iota(jnp.int32, (1, 512), 1) // COLUMNS
    attended = []
    kv_copy.wait()
    for rel in range(FRAMES):
        frame = (2 * yl + c) ^ rel
        mine = projected[rel * COLUMNS : (rel + 1) * COLUMNS]
        fresh = mine[:, 192:]
        fresh_ref[frame] = fresh
        query = mine[:, :192]
        zero = jnp.zeros_like(query)
        queries = jnp.concatenate([jnp.where(head_of == h, query, zero) for h in range(3)], axis=0)
        blocks = [fresh]
        for half in range(2):
            start = pl.multiple_of(half * 64 + frame * COLUMNS, COLUMNS)
            blocks.append(kv_scr[:, pl.ds(start, COLUMNS), :].reshape(512, 384))
        scores = [
            lax.dot_general(queries, b[:, :192], NT, preferred_element_type=F32) * score_scale
            for b in blocks
        ]
        scores[1] = jnp.where(key_row == place, -jnp.inf, scores[1])
        top = jnp.max(scores[0], axis=-1, keepdims=True)
        for s in scores[1:]:
            top = jnp.maximum(top, jnp.max(s, axis=-1, keepdims=True))
        numerator, total = None, None
        for s, b in zip(scores, blocks):
            expo = jnp.exp(s - top)
            part = jnp.dot(expo.astype(BF16), b[:, 192:], preferred_element_type=F32)
            weight = jnp.sum(expo, axis=-1, keepdims=True)
            numerator = part if numerator is None else numerator + part
            total = weight if total is None else total + weight
        result = numerator / total
        rows = jnp.zeros((COLUMNS, 192), F32)
        for h in range(3):
            rows = jnp.where(head_of == h, result[h * COLUMNS : (h + 1) * COLUMNS], rows)
        attended.append(rows.astype(BF16))
    attended = jnp.concatenate(attended, axis=0)
    part = lax.dot_general(attended, out_weights, NT, preferred_element_type=F32)
    for rel in range(FRAMES):
        target = send_ref if rel % 2 else keep_ref
        target[rel // 2] = part[rel * COLUMNS : (rel + 1) * COLUMNS]


def temporal_kernel(where_ref, *refs):
    pieces, packed_ref = refs[:4], refs[4]
    keep_ref, send_ref, w_scr, w_sem = refs[5:]
    w_copy = pltpu.make_async_copy(packed_ref.at[:, 208:], w_scr, w_sem)
    w_copy.start()
    turn = order_matrix()
    section = jnp.concatenate([p[...] for p in pieces], axis=0)
    sources = []
    for chunk in range(8):
        lhs = jnp.concatenate(
            [section[:, k * 640 + chunk * 80 : k * 640 + chunk * 80 + 80] for k in range(2)], axis=1
        )
        sources.append(lax.dot_general(lhs, turn, NT, preferred_element_type=F32).astype(BF16))
    w_copy.wait()
    temporal = None
    out_weights = []
    for chunk in range(8):
        rhs = chunk_of(w_scr, chunk, range(4))
        part = jnp.dot(sources[chunk], rhs[:, :960], preferred_element_type=F32)
        temporal = part if temporal is None else temporal + part
        out_weights.append(rhs[:, 960:1280])
    temporal = temporal.astype(BF16)
    score_scale = HEAD_DIM ** (-0.5)
    row = lax.broadcasted_iota(jnp.int32, (64, 64), 0) % COLUMNS
    col = lax.broadcasted_iota(jnp.int32, (64, 64), 1) % COLUMNS
    outs = []
    for head in range(5):
        query, key, value = [
            temporal[:, k * 320 + head * 64 : k * 320 + (head + 1) * 64] for k in range(3)
        ]
        scores = lax.dot_general(query, key, NT, preferred_element_type=F32) * score_scale
        expo, total = softmax_parts(jnp.where(row == col, scores, -jnp.inf))
        outs.append(jnp.dot(expo, value, preferred_element_type=F32) / total)
    mixed = jnp.concatenate(outs, axis=1).astype(BF16)
    part = lax.dot_general(
        mixed, reorder_rows(turn, out_weights), NT, preferred_element_type=F32
    )
    for rel in range(FRAMES):
        target = send_ref if rel % 2 else keep_ref
        target[rel // 2] = part[rel * COLUMNS : (rel + 1) * COLUMNS]


def final_kernel(where_ref, *refs):
    out_ref = refs[4]
    mine = 2 * where_ref[0] + where_ref[1]
    for rel in range(FRAMES):
        out_ref[mine ^ rel] = refs[rel][...]


def call(kernel, out_shape, *args, scratch=(), flops=0, smem=False, hbm=None):
    moved = sum(a.size * a.dtype.itemsize for a in args)
    return pl.pallas_call(
        kernel,
        out_shape=out_shape,
        in_specs=[
            SMEM if smem and i == 0 else HBM if i == hbm else VMEM for i in range(len(args))
        ],
        out_specs=jax.tree.map(lambda _: VMEM, out_shape),
        scratch_shapes=list(scratch),
        compiler_params=PARAMS,
        cost_estimate=pl.CostEstimate(flops=flops, bytes_accessed=moved, transcendentals=0),
    )(*args)


def shape(dims, dtype):
    return jax.ShapeDtypeStruct(dims, dtype)


def swap(value, axis):
    return lax.ppermute(value, axis, [(0, 1), (1, 0)])


def sum_over_frame(keep, send):
    got = swap(send, "c")
    away = keep[1] + got[1]
    return keep[0] + got[0], swap(away, "yl")


def gather_frame(piece):
    other = swap(piece, "c")
    return [piece, other, swap(piece, "yl"), swap(other, "yl")]


def shards(
    latent,
    stale_latent,
    conv_weight,
    temb_table,
    step_index,
    gn_gain,
    gn_shift,
    w_sqkv,
    stale_kv,
    w_sout,
    w_tqkv,
    w_tout,
):
    yl, c, yh, z, x = (lax.axis_index(a) for a in ("yl", "c", "yh", "z", "x"))
    where = jnp.stack([yl, c, z, yh, x]).astype(jnp.int32)

    count = 64
    above = lax.ppermute(stale_latent, PATCH, [(i, i + 1) for i in range(count - 1)])
    below = lax.ppermute(stale_latent, PATCH, [(i + 1, i) for i in range(count - 1)])
    conv_block = jnp.transpose(conv_weight, (2, 0, 1)).reshape(20, 9 * 320)
    conv_parts = gather_x(pair_yh(conv_block, yh), x)
    conv_full = jnp.concatenate(conv_parts, axis=0)

    weights = jnp.concatenate(
        [
            w_sqkv.reshape(20, 576),
            w_sout.T,
            w_tqkv.reshape(20, 960),
            w_tout.T,
            jnp.zeros((20, 256), BF16),
        ],
        axis=1,
    )
    kv = stale_kv.reshape(FRAMES * COLUMNS, 384)
    kv_other = from_shift(kv, "yh", 1)
    weights = pair_yh(weights, yh)
    weights = [weights[:, k * 384 : (k + 1) * 384] for k in range(6)]
    packed = jnp.concatenate([kv, kv_other] + weights, axis=0)
    packed = lax.all_gather(packed, ("z", "x"), axis=0, tiled=False)

    rows = jnp.concatenate([above, latent, below], axis=1).transpose(1, 0, 2, 3)
    rows = lax.all_to_all(jnp.broadcast_to(rows, (8,) + rows.shape), "z", 0, 0)
    half = shape((2, 128, 160), F32)
    keep, send = call(conv_kernel, (half, half), where, rows, conv_full, smem=True, flops=3 * 10**9)
    mine, got = sum_over_frame(keep, send)

    def channels_of(vector):
        local = lax.dynamic_index_in_dim(vector.reshape(2, 8, 4, 20), z, 1, keepdims=False)
        return local.transpose(1, 0, 2).reshape(1, 160)

    embed = channels_of(lax.dynamic_index_in_dim(temb_table, step_index[0], 0, keepdims=False))
    hidden, stats = call(
        stats_kernel, (shape((128, 160), F32), shape((8, 128), F32)), mine, got, embed.astype(F32)
    )
    stats = lax.all_to_all(jnp.broadcast_to(stats, (8, 8, 128)), ("yh", "x"), 0, 0)
    activated = call(
        norm_kernel,
        shape((8, COLUMNS, 160), BF16),
        hidden,
        stats,
        channels_of(gn_gain),
        channels_of(gn_shift),
    )
    activated = lax.all_to_all(activated, "z", 0, 0)

    share = shape((2, COLUMNS, CHANNELS), F32)
    keep, send, fresh, own = call(
        spatial_kernel,
        (share, share, shape((FRAMES, COLUMNS, 384), BF16), shape((COLUMNS, CHANNELS), BF16)),
        where,
        *gather_frame(activated),
        packed,
        smem=True,
        hbm=5,
        scratch=[
            pltpu.VMEM((32, 80, 384), BF16),
            pltpu.VMEM((32, 128, 384), BF16),
            pltpu.SemaphoreType.DMA,
            pltpu.SemaphoreType.DMA,
        ],
        flops=10**9,
    )
    mine, got = sum_over_frame(keep, send)
    section = (own.astype(F32) + (mine + got)).astype(BF16)
    keep, send = call(
        temporal_kernel,
        (share, share),
        where,
        *gather_frame(section),
        packed,
        smem=True,
        hbm=5,
        scratch=[pltpu.VMEM((32, 160, 384), BF16), pltpu.SemaphoreType.DMA],
        flops=10**9,
    )
    mine, got = sum_over_frame(keep, send)
    mixed = (section.astype(F32) + (mine + got)).astype(BF16)
    mixed = call(
        final_kernel,
        shape((FRAMES, COLUMNS, CHANNELS), BF16),
        where,
        *gather_frame(mixed),
        smem=True,
    )
    return (
        mixed.reshape(FRAMES, 1, COLUMNS, CHANNELS),
        fresh.reshape(FRAMES, 1, COLUMNS, 2, 192),
    )


def solution(mesh):
    fine = Mesh(mesh.devices.reshape(2, 2, 2, 8, 4), ("yl", "c", "yh", "z", "x"))
    return jax.shard_map(
        shards,
        mesh=fine,
        in_specs=(
            P(None, PATCH, None, FRAME),
            P(None, PATCH, None, FRAME),
            P(None, FRAME, PATCH),
            P(),
            P(),
            P(),
            P(),
            P(PATCH, None, FRAME),
            P(None, PATCH, None, None, FRAME),
            P(FRAME, PATCH),
            P(PATCH, None, FRAME),
            P(FRAME, PATCH),
        ),
        out_specs=(P(None, PATCH, None, None), P(None, PATCH, None, None, FRAME)),
        check_vma=False,
    )
```

```python
import jax
import jax.numpy as jnp
from jax import lax
from jax.experimental import pallas as pl
from jax.experimental.pallas import tpu as pltpu
from jax.sharding import Mesh
from jax.sharding import PartitionSpec as P

CHANNELS = 1280
GROUPS = 32
GROUP_WIDTH = CHANNELS // GROUPS
HEAD_DIM = 64
FRAMES = 4
COLUMNS = 16
SIZES = {"yl": 2, "c": 2, "yh": 2, "z": 8, "x": 4}
FRAME = ("yl", "c")
PATCH = ("yh", "z", "x")
RING = (0, 1, 7, 2, 6, 3, 5, 4)
BF16 = jnp.bfloat16
F32 = jnp.float32
VMEM = pl.BlockSpec(memory_space=pltpu.VMEM)
SMEM = pl.BlockSpec(memory_space=pltpu.SMEM)
HBM = pl.BlockSpec(memory_space=pltpu.HBM)
NT = (((1,), (1,)), ((), ()))


def from_shift(value, axis, offset):
    size = SIZES[axis]
    return lax.ppermute(value, axis, [((i + offset) % size, i) for i in range(size)])


def ring_gather(block):
    ahead, behind = [block], [block]
    for _ in range(3):
        ahead.append(from_shift(ahead[-1], "z", 1))
        behind.append(from_shift(behind[-1], "z", -1))
    far = from_shift(ahead[-1], "z", 1)
    return [block, ahead[1], behind[1], ahead[2], behind[2], ahead[3], behind[3], far]


def pair_yh(block, yh):
    other = from_shift(block, "yh", 1)
    return jnp.concatenate(
        [jnp.where(yh == 0, block, other), jnp.where(yh == 0, other, block)], axis=0
    )


def gather_x(pair, x):
    parts = [pair] + [from_shift(pair, "x", k) for k in (1, 2, 3)]
    ordered = []
    for place in range(4):
        chosen = parts[place]
        for mine in (1, 2, 3):
            chosen = jnp.where(x == mine, parts[(place - mine) % 4], chosen)
        ordered.append(chosen)
    return ordered


def conv_kernel(where_ref, *refs):
    rows_refs, weight_ref, keep_ref, send_ref = refs[:8], refs[8], refs[9], refs[10]
    yl, c, z = where_ref[0], where_ref[1], where_ref[2]
    column = lax.broadcasted_iota(jnp.int32, (512, 1), 0) % COLUMNS
    sums = []
    for col_tap in range(3):
        total = None
        for row_tap in range(3):
            lhs = jnp.concatenate([r[row_tap] for r in rows_refs], axis=0)
            tap = 3 * row_tap + col_tap
            part = lax.dot_general(
                lhs,
                weight_ref[:, tap * 320 : (tap + 1) * 320],
                NT,
                preferred_element_type=F32,
            )
            total = part if total is None else total + part
        sums.append(total)
    left = jnp.where(column == 0, 0.0, pltpu.roll(sums[0], 1, 0))
    right = jnp.where(column == COLUMNS - 1, 0.0, pltpu.roll(sums[2], 511, 0))
    hidden = (sums[1] + left + right).reshape(8, FRAMES, COLUMNS, 160)
    for k, offset in enumerate(RING):
        start = pl.multiple_of((z + offset) % 8 * COLUMNS, COLUMNS)
        for frame in range(FRAMES):
            value = hidden[k, frame]
            place = yl ^ (frame // 2)

            @pl.when(c == frame % 2)
            def _():
                keep_ref[place, pl.ds(start, COLUMNS)] = value

            @pl.when(c != frame % 2)
            def _():
                send_ref[place, pl.ds(start, COLUMNS)] = value


def group_masks():
    lane = lax.broadcasted_iota(jnp.int32, (1, 160), 1)
    return [(lane // 80) * 2 + (lane % 40) // 20 == g for g in range(4)]


def stats_kernel(keep_ref, got_ref, embed_ref, hidden_ref, stats_ref):
    hidden = keep_ref[...] + got_ref[...] + embed_ref[...]
    hidden_ref[...] = hidden
    count = 128.0 * GROUP_WIDTH
    masks = group_masks()
    sums = jnp.sum(hidden, axis=0, keepdims=True)
    means = [jnp.sum(jnp.where(m, sums, 0.0), axis=1, keepdims=True) / count for m in masks]
    mean = sum(jnp.where(m, v, 0.0) for m, v in zip(masks, means))
    centred = hidden - mean
    squares = jnp.sum(centred * centred, axis=0, keepdims=True)
    lane = lax.broadcasted_iota(jnp.int32, (8, 128), 1)
    out = jnp.zeros((8, 128), F32)
    for g in range(4):
        spread = jnp.sum(jnp.where(masks[g], squares, 0.0), axis=1, keepdims=True)
        out = jnp.where(lane == g, means[g], out)
        out = jnp.where(lane == 4 + g, spread, out)
    stats_ref[...] = out


def norm_kernel(hidden_ref, stats_ref, gain_ref, shift_ref, out_ref):
    stats = stats_ref[...]
    masks = group_masks()
    local = 128.0 * GROUP_WIDTH
    mean_row = jnp.zeros((1, 160), F32)
    scale_row = jnp.zeros((1, 160), F32)
    for g in range(4):
        means = stats[:, 0:1, g : g + 1]
        mean = jnp.sum(means, axis=0, keepdims=True) / 8.0
        gap = means - mean
        spread = jnp.sum(stats[:, 0:1, 4 + g : 5 + g] + local * gap * gap, axis=0) / (8.0 * local)
        mean_row = jnp.where(masks[g], mean[0], mean_row)
        scale_row = jnp.where(masks[g], lax.rsqrt(spread + 1e-05), scale_row)
    normed = (hidden_ref[...] - mean_row) * scale_row
    value = normed * gain_ref[...] + shift_ref[...]
    out_ref[...] = jax.nn.silu(value).astype(BF16).reshape(8, COLUMNS, 160)


def softmax_parts(scores):
    top = jnp.max(scores, axis=-1, keepdims=True)
    expo = jnp.exp(scores - top)
    return expo.astype(BF16), jnp.sum(expo, axis=-1, keepdims=True)


def order_matrix():
    row = lax.broadcasted_iota(jnp.int32, (160, 160), 0)
    col = lax.broadcasted_iota(jnp.int32, (160, 160), 1)
    return (row // 40 * 20 + row % 20 + (row % 40) // 20 * 80 == col).astype(BF16)


def reorder_rows(turn, chunks):
    turned = []
    for rows in chunks:
        value = lax.dot_general(turn, rows, (((0,), (0,)), ((), ())), preferred_element_type=F32)
        turned.append(value.astype(BF16))
    return jnp.concatenate([t[80 * h : 80 * h + 80] for h in range(2) for t in turned], axis=0)


def chunk_of(w_ref, chunk, blocks):
    places = slice(4 * chunk, 4 * chunk + 4)
    parts = [w_ref[places, 40 * k : 40 * k + 40, :].reshape(160, 256) for k in blocks]
    return jnp.concatenate(parts, axis=1)


def spatial_kernel(where_ref, *refs):
    acts, packed_ref = refs[:4], refs[4]
    out_ref, fresh_ref, own_ref, w_scr, kv_scr, w_sem, kv_sem = refs[5:]
    w_copy = pltpu.make_async_copy(packed_ref.at[:, 192:312], w_scr, w_sem)
    kv_copy = pltpu.make_async_copy(packed_ref.at[:, :192], kv_scr, kv_sem)
    w_copy.start()
    kv_copy.start()
    yl, c, place = where_ref[0], where_ref[1], where_ref[2] * 4 + where_ref[4]
    turn = order_matrix()
    frames = [(2 * yl + c) ^ rel for rel in range(FRAMES)]
    sources = [jnp.concatenate([a[chunk] for a in acts], axis=0) for chunk in range(8)]
    own = [jnp.dot(v, turn, preferred_element_type=F32).astype(BF16) for v in sources]
    own = jnp.concatenate([o[:, 80 * h : 80 * h + 80] for h in range(2) for o in own], axis=1)
    for rel, frame in enumerate(frames):
        own_ref[frame] = own[rel * COLUMNS : (rel + 1) * COLUMNS]
    w_copy.wait()
    projected = None
    out_weights = []
    for chunk in range(8):
        rhs = chunk_of(w_scr, chunk, range(3))
        part = jnp.dot(sources[chunk], rhs[:, :576], preferred_element_type=F32)
        projected = part if projected is None else projected + part
        out_weights.append(rhs[:, 576:])
    projected = projected.astype(BF16)
    out_weights = reorder_rows(turn, out_weights)
    score_scale = HEAD_DIM ** (-0.5)
    head_of = lax.broadcasted_iota(jnp.int32, (COLUMNS, 192), 1) // HEAD_DIM
    key_row = lax.broadcasted_iota(jnp.int32, (1, 512), 1) // COLUMNS
    attended = []
    kv_copy.wait()
    for rel, frame in enumerate(frames):
        mine = projected[rel * COLUMNS : (rel + 1) * COLUMNS]
        fresh = mine[:, 192:]
        fresh_ref[frame] = fresh
        query = mine[:, :192]
        zero = jnp.zeros_like(query)
        queries = jnp.concatenate([jnp.where(head_of == h, query, zero) for h in range(3)], axis=0)
        start = pl.multiple_of(frame * COLUMNS, COLUMNS)
        low, high = [], []
        for half in range(2):
            rows = pl.ds(half * 64 + start, COLUMNS)
            low.append(kv_scr[:, rows, :].reshape(512, 256))
            rows = pl.ds(128 + start, COLUMNS)
            high.append(kv_scr[:, rows, half * 128 : half * 128 + 128].reshape(512, 128))
        scores = [lax.dot_general(queries, fresh[:, :192], NT, preferred_element_type=F32)]
        for a, b in zip(low, high):
            far = lax.dot_general(queries[:, :128], a[:, :128], NT, preferred_element_type=F32)
            scores.append(
                far
                + lax.dot_general(queries[:, 128:], b[:, :64], NT, preferred_element_type=F32)
            )
        scores = [s * score_scale for s in scores]
        scores[1] = jnp.where(key_row == place, -jnp.inf, scores[1])
        top = jnp.max(scores[0], axis=-1, keepdims=True)
        for s in scores[1:]:
            top = jnp.maximum(top, jnp.max(s, axis=-1, keepdims=True))
        expo = [jnp.exp(s - top) for s in scores]
        total = sum(jnp.sum(e, axis=-1, keepdims=True) for e in expo)
        expo = [e.astype(BF16) for e in expo]
        numerator = jnp.dot(expo[0], fresh[:, 192:], preferred_element_type=F32)
        for e, a, b in zip(expo[1:], low, high):
            values = jnp.concatenate([a[:, 128:], b[:, 64:]], axis=1)
            numerator = numerator + jnp.dot(e, values, preferred_element_type=F32)
        result = numerator / total
        rows = jnp.zeros((COLUMNS, 192), F32)
        for h in range(3):
            rows = jnp.where(head_of == h, result[h * COLUMNS : (h + 1) * COLUMNS], rows)
        attended.append(rows.astype(BF16))
    attended = jnp.concatenate(attended, axis=0)
    part = lax.dot_general(attended, out_weights, NT, preferred_element_type=F32)
    for rel, frame in enumerate(frames):
        out_ref[frame] = part[rel * COLUMNS : (rel + 1) * COLUMNS]


def temporal_kernel(own_ref, mine_ref, got_ref, packed_ref, out_ref, section_ref):
    turn = order_matrix()
    total = mine_ref[...].astype(F32) + got_ref[...].astype(F32)
    section = (own_ref[...].astype(F32) + total).astype(BF16)
    section_ref[...] = section
    section = section.reshape(64, CHANNELS)
    sources = []
    for chunk in range(8):
        lhs = jnp.concatenate(
            [section[:, k * 640 + chunk * 80 : k * 640 + chunk * 80 + 80] for k in range(2)], axis=1
        )
        sources.append(lax.dot_general(lhs, turn, NT, preferred_element_type=F32).astype(BF16))
    temporal = None
    out_weights = []
    for chunk in range(8):
        rhs = chunk_of(packed_ref, chunk, range(5))
        part = jnp.dot(sources[chunk], rhs[:, :960], preferred_element_type=F32)
        temporal = part if temporal is None else temporal + part
        out_weights.append(rhs[:, 960:])
    temporal = temporal.astype(BF16)
    score_scale = HEAD_DIM ** (-0.5)
    row = lax.broadcasted_iota(jnp.int32, (64, 64), 0) % COLUMNS
    col = lax.broadcasted_iota(jnp.int32, (64, 64), 1) % COLUMNS
    outs = []
    for head in range(5):
        query, key, value = [
            temporal[:, k * 320 + head * 64 : k * 320 + (head + 1) * 64] for k in range(3)
        ]
        scores = lax.dot_general(query, key, NT, preferred_element_type=F32) * score_scale
        expo, total = softmax_parts(jnp.where(row == col, scores, -jnp.inf))
        outs.append(jnp.dot(expo, value, preferred_element_type=F32) / total)
    mixed = jnp.concatenate(outs, axis=1).astype(BF16)
    part = lax.dot_general(
        mixed, reorder_rows(turn, out_weights), NT, preferred_element_type=F32
    )
    out_ref[...] = part.reshape(FRAMES, COLUMNS, CHANNELS)


def call(kernel, out_shape, *args, scratch=(), flops=0, smem=False, hbm=(), limit=40):
    moved = sum(a.size * a.dtype.itemsize for a in args)
    return pl.pallas_call(
        kernel,
        out_shape=out_shape,
        in_specs=[
            SMEM if smem and i == 0 else HBM if i in hbm else VMEM for i in range(len(args))
        ],
        out_specs=jax.tree.map(lambda _: VMEM, out_shape),
        scratch_shapes=list(scratch),
        compiler_params=pltpu.CompilerParams(vmem_limit_bytes=limit * 1024 * 1024),
        cost_estimate=pl.CostEstimate(flops=flops, bytes_accessed=moved, transcendentals=0),
    )(*args)


def shape(dims, dtype):
    return jax.ShapeDtypeStruct(dims, dtype)


def swap(value, axis):
    return lax.ppermute(value, axis, [(0, 1), (1, 0)])


def sum_over_frame(keep, send):
    got = swap(send, "c")
    away = keep[1] + got[1]
    return keep[0] + got[0], swap(away, "yl")


def sum_both(part):
    mine = (part + swap(part, "c")).astype(BF16)
    return mine, swap(mine, "yl")


def gather_frame(piece):
    other = swap(piece, "c")
    return [piece, other, swap(piece, "yl"), swap(other, "yl")]


def shards(
    latent,
    stale_latent,
    conv_weight,
    temb_table,
    step_index,
    gn_gain,
    gn_shift,
    w_sqkv,
    stale_kv,
    w_sout,
    w_tqkv,
    w_tout,
):
    yl, c, yh, z, x = (lax.axis_index(a) for a in ("yl", "c", "yh", "z", "x"))
    where = jnp.stack([yl, c, z, yh, x]).astype(jnp.int32)

    count = 64
    above = lax.ppermute(stale_latent, PATCH, [(i, i + 1) for i in range(count - 1)])
    below = lax.ppermute(stale_latent, PATCH, [(i + 1, i) for i in range(count - 1)])
    conv_block = jnp.transpose(conv_weight, (2, 0, 1)).reshape(20, 9 * 320)
    conv_parts = gather_x(pair_yh(conv_block, yh), x)
    conv_full = jnp.concatenate(conv_parts, axis=0)

    weights = jnp.concatenate(
        [
            w_sqkv.reshape(20, 576),
            w_sout.T,
            w_tqkv.reshape(20, 960),
            w_tout.T,
        ],
        axis=1,
    )
    keys, values = [stale_kv[:, :, :, k].reshape(FRAMES * COLUMNS, 192) for k in range(2)]
    kv = jnp.concatenate(
        [keys[:, :128], values[:, :128], keys[:, 128:], values[:, 128:]], axis=1
    )
    kv_other = from_shift(kv, "yh", 1)
    kv = [kv[:, :256], kv_other[:, :256], jnp.concatenate([kv[:, 256:], kv_other[:, 256:]], axis=1)]
    weights = pair_yh(weights, yh)
    weights = [weights[:, k * 256 : (k + 1) * 256] for k in range(8)]
    packed = jnp.concatenate(kv + weights, axis=0)
    packed = lax.all_gather(packed, ("z", "x"), axis=0, tiled=False)

    rows = jnp.concatenate([above, latent, below], axis=1).transpose(1, 0, 2, 3)
    rows = ring_gather(rows.reshape(3, FRAMES * COLUMNS, 320))
    half = shape((2, 128, 160), F32)
    keep, send = call(conv_kernel, (half, half), where, *rows, conv_full, smem=True, flops=3 * 10**9)
    mine, got = sum_over_frame(keep, send)

    def channels_of(vector):
        local = lax.dynamic_index_in_dim(vector.reshape(2, 8, 4, 20), z, 1, keepdims=False)
        return local.transpose(1, 0, 2).reshape(1, 160)

    embed = channels_of(lax.dynamic_index_in_dim(temb_table, step_index[0], 0, keepdims=False))
    hidden, stats = call(
        stats_kernel, (shape((128, 160), F32), shape((8, 128), F32)), mine, got, embed.astype(F32)
    )
    stats = lax.all_to_all(jnp.broadcast_to(stats, (8, 8, 128)), ("yh", "x"), 0, 0)
    activated = call(
        norm_kernel,
        shape((8, COLUMNS, 160), BF16),
        hidden,
        stats,
        channels_of(gn_gain),
        channels_of(gn_shift),
    )
    activated = lax.all_to_all(activated, "z", 0, 0)

    full = (FRAMES, COLUMNS, CHANNELS)
    part, fresh, own = call(
        spatial_kernel,
        (shape(full, F32), shape((FRAMES, COLUMNS, 384), BF16), shape(full, BF16)),
        where,
        *gather_frame(activated),
        packed,
        smem=True,
        hbm=(5,),
        limit=56,
        scratch=[
            pltpu.VMEM((32, 120, 256), BF16),
            pltpu.VMEM((32, 192, 256), BF16),
            pltpu.SemaphoreType.DMA,
            pltpu.SemaphoreType.DMA,
        ],
        flops=10**9,
    )
    packed, part = lax.optimization_barrier((packed, part))
    second = packed[:, 312:]
    part, section = call(
        temporal_kernel,
        (shape(full, F32), shape(full, BF16)),
        own,
        *sum_both(part),
        second,
        flops=10**9,
    )
    mine, got = sum_both(part)
    mixed = (section.astype(F32) + (mine.astype(F32) + got.astype(F32))).astype(BF16)
    return (
        mixed.reshape(FRAMES, 1, COLUMNS, CHANNELS),
        fresh.reshape(FRAMES, 1, COLUMNS, 2, 192),
    )


def solution(mesh):
    fine = Mesh(mesh.devices.reshape(2, 2, 2, 8, 4), ("yl", "c", "yh", "z", "x"))
    return jax.shard_map(
        shards,
        mesh=fine,
        in_specs=(
            P(None, PATCH, None, FRAME),
            P(None, PATCH, None, FRAME),
            P(None, FRAME, PATCH),
            P(),
            P(),
            P(),
            P(),
            P(PATCH, None, FRAME),
            P(None, PATCH, None, None, FRAME),
            P(FRAME, PATCH),
            P(PATCH, None, FRAME),
            P(FRAME, PATCH),
        ),
        out_specs=(P(None, PATCH, None, None), P(None, PATCH, None, None, FRAME)),
        check_vma=False,
    )
```

```python
import jax
import jax.numpy as jnp
from jax import lax
from jax.experimental import pallas as pl
from jax.experimental.pallas import tpu as pltpu
from jax.sharding import Mesh
from jax.sharding import PartitionSpec as P

CHANNELS = 1280
GROUPS = 32
GROUP_WIDTH = CHANNELS // GROUPS
HEAD_DIM = 64
FRAMES = 4
COLUMNS = 16
SIZES = {"yl": 2, "c": 2, "yh": 2, "z": 8, "x": 4}
FRAME = ("yl", "c")
PATCH = ("yh", "z", "x")
RING = (0, 1, 7, 2, 6, 3, 5, 4)
BF16 = jnp.bfloat16
F32 = jnp.float32
VMEM = pl.BlockSpec(memory_space=pltpu.VMEM)
SMEM = pl.BlockSpec(memory_space=pltpu.SMEM)
HBM = pl.BlockSpec(memory_space=pltpu.HBM)
NT = (((1,), (1,)), ((), ()))


def from_shift(value, axis, offset):
    size = SIZES[axis]
    return lax.ppermute(value, axis, [((i + offset) % size, i) for i in range(size)])


def ring_gather(block):
    ahead, behind = [block], [block]
    for _ in range(3):
        ahead.append(from_shift(ahead[-1], "z", 1))
        behind.append(from_shift(behind[-1], "z", -1))
    far = from_shift(ahead[-1], "z", 1)
    return [block, ahead[1], behind[1], ahead[2], behind[2], ahead[3], behind[3], far]


def pair_yh(block, yh):
    other = from_shift(block, "yh", 1)
    return jnp.concatenate(
        [jnp.where(yh == 0, block, other), jnp.where(yh == 0, other, block)], axis=0
    )


def gather_x(pair, x):
    parts = [pair] + [from_shift(pair, "x", k) for k in (1, 2, 3)]
    ordered = []
    for place in range(4):
        chosen = parts[place]
        for mine in (1, 2, 3):
            chosen = jnp.where(x == mine, parts[(place - mine) % 4], chosen)
        ordered.append(chosen)
    return ordered


def conv_kernel(where_ref, *refs):
    rows_refs, weight_ref, keep_ref, send_ref = refs[:8], refs[8], refs[9], refs[10]
    yl, c, z = where_ref[0], where_ref[1], where_ref[2]
    column = lax.broadcasted_iota(jnp.int32, (512, 1), 0) % COLUMNS
    sums = []
    for col_tap in range(3):
        total = None
        for row_tap in range(3):
            lhs = jnp.concatenate([r[row_tap] for r in rows_refs], axis=0)
            tap = 3 * row_tap + col_tap
            part = lax.dot_general(
                lhs,
                weight_ref[:, tap * 320 : (tap + 1) * 320],
                NT,
                preferred_element_type=F32,
            )
            total = part if total is None else total + part
        sums.append(total)
    left = jnp.where(column == 0, 0.0, pltpu.roll(sums[0], 1, 0))
    right = jnp.where(column == COLUMNS - 1, 0.0, pltpu.roll(sums[2], 511, 0))
    hidden = (sums[1] + left + right).reshape(8, FRAMES, COLUMNS, 160)
    for k, offset in enumerate(RING):
        start = pl.multiple_of((z + offset) % 8 * COLUMNS, COLUMNS)
        for frame in range(FRAMES):
            value = hidden[k, frame]
            place = yl ^ (frame // 2)

            @pl.when(c == frame % 2)
            def _():
                keep_ref[place, pl.ds(start, COLUMNS)] = value

            @pl.when(c != frame % 2)
            def _():
                send_ref[place, pl.ds(start, COLUMNS)] = value


def group_masks():
    lane = lax.broadcasted_iota(jnp.int32, (1, 160), 1)
    return [(lane // 80) * 2 + (lane % 40) // 20 == g for g in range(4)]


def stats_kernel(keep_ref, got_ref, embed_ref, hidden_ref, stats_ref):
    hidden = keep_ref[...] + got_ref[...] + embed_ref[...]
    hidden_ref[...] = hidden
    count = 128.0 * GROUP_WIDTH
    masks = group_masks()
    sums = jnp.sum(hidden, axis=0, keepdims=True)
    means = [jnp.sum(jnp.where(m, sums, 0.0), axis=1, keepdims=True) / count for m in masks]
    mean = sum(jnp.where(m, v, 0.0) for m, v in zip(masks, means))
    centred = hidden - mean
    squares = jnp.sum(centred * centred, axis=0, keepdims=True)
    lane = lax.broadcasted_iota(jnp.int32, (8, 128), 1)
    out = jnp.zeros((8, 128), F32)
    for g in range(4):
        spread = jnp.sum(jnp.where(masks[g], squares, 0.0), axis=1, keepdims=True)
        out = jnp.where(lane == g, means[g], out)
        out = jnp.where(lane == 4 + g, spread, out)
    stats_ref[...] = out


def norm_kernel(hidden_ref, stats_ref, gain_ref, shift_ref, out_ref):
    stats = stats_ref[...]
    masks = group_masks()
    local = 128.0 * GROUP_WIDTH
    mean_row = jnp.zeros((1, 160), F32)
    scale_row = jnp.zeros((1, 160), F32)
    for g in range(4):
        means = stats[:, 0:1, g : g + 1]
        mean = jnp.sum(means, axis=0, keepdims=True) / 8.0
        gap = means - mean
        spread = jnp.sum(stats[:, 0:1, 4 + g : 5 + g] + local * gap * gap, axis=0) / (8.0 * local)
        mean_row = jnp.where(masks[g], mean[0], mean_row)
        scale_row = jnp.where(masks[g], lax.rsqrt(spread + 1e-05), scale_row)
    normed = (hidden_ref[...] - mean_row) * scale_row
    value = normed * gain_ref[...] + shift_ref[...]
    out_ref[...] = jax.nn.silu(value).astype(BF16).reshape(8, COLUMNS, 160)


def softmax_parts(scores):
    top = jnp.max(scores, axis=-1, keepdims=True)
    expo = jnp.exp(scores - top)
    return expo.astype(BF16), jnp.sum(expo, axis=-1, keepdims=True)


def order_matrix():
    row = lax.broadcasted_iota(jnp.int32, (160, 160), 0)
    col = lax.broadcasted_iota(jnp.int32, (160, 160), 1)
    return (row // 40 * 20 + row % 20 + (row % 40) // 20 * 80 == col).astype(BF16)


def reorder_rows(turn, chunks):
    turned = []
    for rows in chunks:
        value = lax.dot_general(turn, rows, (((0,), (0,)), ((), ())), preferred_element_type=F32)
        turned.append(value.astype(BF16))
    return jnp.concatenate([t[80 * h : 80 * h + 80] for h in range(2) for t in turned], axis=0)


def chunk_of(w_ref, chunk, blocks):
    places = slice(4 * chunk, 4 * chunk + 4)
    parts = [w_ref[places, 40 * k : 40 * k + 40, :].reshape(160, 256) for k in blocks]
    return jnp.concatenate(parts, axis=1)


def spatial_kernel(where_ref, *refs):
    acts, packed_ref = refs[:4], refs[4]
    out_ref, fresh_ref, own_ref, w_scr, kv_scr, w_sem, kv_sem = refs[5:]
    w_copy = pltpu.make_async_copy(packed_ref.at[:, 192:312], w_scr, w_sem)
    kv_copy = pltpu.make_async_copy(packed_ref.at[:, :192], kv_scr, kv_sem)
    w_copy.start()
    kv_copy.start()
    yl, c, place = where_ref[0], where_ref[1], where_ref[2] * 4 + where_ref[4]
    frames = [(2 * yl + c) ^ rel for rel in range(FRAMES)]
    sources = [jnp.concatenate([a[chunk] for a in acts], axis=0) for chunk in range(8)]
    own = jnp.concatenate(sources, axis=1)
    for rel, frame in enumerate(frames):
        own_ref[frame] = own[rel * COLUMNS : (rel + 1) * COLUMNS]
    w_copy.wait()
    projected = None
    out_weights = []
    for chunk in range(8):
        rhs = chunk_of(w_scr, chunk, range(3))
        part = jnp.dot(sources[chunk], rhs[:, :576], preferred_element_type=F32)
        projected = part if projected is None else projected + part
        out_weights.append(rhs[:, 576:])
    projected = projected.astype(BF16)
    out_weights = jnp.concatenate(out_weights, axis=0)
    score_scale = HEAD_DIM ** (-0.5)
    head_of = lax.broadcasted_iota(jnp.int32, (COLUMNS, 192), 1) // HEAD_DIM
    key_row = lax.broadcasted_iota(jnp.int32, (1, 512), 1) // COLUMNS
    attended = []
    kv_copy.wait()
    for rel, frame in enumerate(frames):
        mine = projected[rel * COLUMNS : (rel + 1) * COLUMNS]
        fresh = mine[:, 192:]
        fresh_ref[frame] = fresh
        query = mine[:, :192]
        zero = jnp.zeros_like(query)
        queries = jnp.concatenate([jnp.where(head_of == h, query, zero) for h in range(3)], axis=0)
        start = pl.multiple_of(frame * COLUMNS, COLUMNS)
        low, high = [], []
        for half in range(2):
            rows = pl.ds(half * 64 + start, COLUMNS)
            low.append(kv_scr[:, rows, :].reshape(512, 256))
            rows = pl.ds(128 + start, COLUMNS)
            high.append(kv_scr[:, rows, half * 128 : half * 128 + 128].reshape(512, 128))
        scores = [lax.dot_general(queries, fresh[:, :192], NT, preferred_element_type=F32)]
        for a, b in zip(low, high):
            far = lax.dot_general(queries[:, :128], a[:, :128], NT, preferred_element_type=F32)
            scores.append(
                far
                + lax.dot_general(queries[:, 128:], b[:, :64], NT, preferred_element_type=F32)
            )
        scores = [s * score_scale for s in scores]
        scores[1] = jnp.where(key_row == place, -jnp.inf, scores[1])
        top = jnp.max(scores[0], axis=-1, keepdims=True)
        for s in scores[1:]:
            top = jnp.maximum(top, jnp.max(s, axis=-1, keepdims=True))
        expo = [jnp.exp(s - top) for s in scores]
        total = sum(jnp.sum(e, axis=-1, keepdims=True) for e in expo)
        expo = [e.astype(BF16) for e in expo]
        numerator = jnp.dot(expo[0], fresh[:, 192:], preferred_element_type=F32)
        for e, a, b in zip(expo[1:], low, high):
            values = jnp.concatenate([a[:, 128:], b[:, 64:]], axis=1)
            numerator = numerator + jnp.dot(e, values, preferred_element_type=F32)
        result = numerator / total
        rows = jnp.zeros((COLUMNS, 192), F32)
        for h in range(3):
            rows = jnp.where(head_of == h, result[h * COLUMNS : (h + 1) * COLUMNS], rows)
        attended.append(rows.astype(BF16))
    attended = jnp.concatenate(attended, axis=0)
    part = lax.dot_general(attended, out_weights, NT, preferred_element_type=F32)
    for rel, frame in enumerate(frames):
        out_ref[frame] = part[rel * COLUMNS : (rel + 1) * COLUMNS].astype(BF16)


def temporal_kernel(own_ref, mine_ref, got_ref, packed_ref, out_ref, section_ref):
    total = mine_ref[...].astype(F32) + got_ref[...].astype(F32)
    section = (own_ref[...].astype(F32) + total).astype(BF16).reshape(64, CHANNELS)
    sources = [section[:, chunk * 160 : (chunk + 1) * 160] for chunk in range(8)]
    temporal = None
    out_weights = []
    for chunk in range(8):
        rhs = chunk_of(packed_ref, chunk, range(5))
        part = jnp.dot(sources[chunk], rhs[:, :960], preferred_element_type=F32)
        temporal = part if temporal is None else temporal + part
        out_weights.append(rhs[:, 960:])
    temporal = temporal.astype(BF16)
    score_scale = HEAD_DIM ** (-0.5)
    row = lax.broadcasted_iota(jnp.int32, (64, 64), 0) % COLUMNS
    col = lax.broadcasted_iota(jnp.int32, (64, 64), 1) % COLUMNS
    outs = []
    for head in range(5):
        query, key, value = [
            temporal[:, k * 320 + head * 64 : k * 320 + (head + 1) * 64] for k in range(3)
        ]
        scores = lax.dot_general(query, key, NT, preferred_element_type=F32) * score_scale
        expo, total = softmax_parts(jnp.where(row == col, scores, -jnp.inf))
        outs.append(jnp.dot(expo, value, preferred_element_type=F32) / total)
    mixed = jnp.concatenate(outs, axis=1).astype(BF16)
    turn = order_matrix()
    turned = [jnp.dot(v, turn, preferred_element_type=F32).astype(BF16) for v in sources]
    turned = jnp.concatenate([t[:, 80 * h : 80 * h + 80] for h in range(2) for t in turned], axis=1)
    section_ref[...] = turned.reshape(FRAMES, COLUMNS, CHANNELS)
    part = lax.dot_general(
        mixed, reorder_rows(turn, out_weights), NT, preferred_element_type=F32
    )
    out_ref[...] = part.astype(BF16).reshape(FRAMES, COLUMNS, CHANNELS)


def call(kernel, out_shape, *args, scratch=(), flops=0, smem=False, hbm=(), limit=40):
    moved = sum(a.size * a.dtype.itemsize for a in args)
    return pl.pallas_call(
        kernel,
        out_shape=out_shape,
        in_specs=[
            SMEM if smem and i == 0 else HBM if i in hbm else VMEM for i in range(len(args))
        ],
        out_specs=jax.tree.map(lambda _: VMEM, out_shape),
        scratch_shapes=list(scratch),
        compiler_params=pltpu.CompilerParams(vmem_limit_bytes=limit * 1024 * 1024),
        cost_estimate=pl.CostEstimate(flops=flops, bytes_accessed=moved, transcendentals=0),
    )(*args)


def shape(dims, dtype):
    return jax.ShapeDtypeStruct(dims, dtype)


def swap(value, axis):
    return lax.ppermute(value, axis, [(0, 1), (1, 0)])


def sum_over_frame(keep, send):
    got = swap(send, "c")
    away = keep[1] + got[1]
    return keep[0] + got[0], swap(away, "yl")


def sum_both(part):
    mine = (part.astype(F32) + swap(part, "c").astype(F32)).astype(BF16)
    return mine, swap(mine, "yl")


def gather_frame(piece):
    other = swap(piece, "c")
    return [piece, other, swap(piece, "yl"), swap(other, "yl")]


def shards(
    latent,
    stale_latent,
    conv_weight,
    temb_table,
    step_index,
    gn_gain,
    gn_shift,
    w_sqkv,
    stale_kv,
    w_sout,
    w_tqkv,
    w_tout,
):
    yl, c, yh, z, x = (lax.axis_index(a) for a in ("yl", "c", "yh", "z", "x"))
    where = jnp.stack([yl, c, z, yh, x]).astype(jnp.int32)

    count = 64
    above = lax.ppermute(stale_latent, PATCH, [(i, i + 1) for i in range(count - 1)])
    below = lax.ppermute(stale_latent, PATCH, [(i + 1, i) for i in range(count - 1)])
    conv_block = jnp.transpose(conv_weight, (2, 0, 1)).reshape(20, 9 * 320)
    conv_parts = gather_x(pair_yh(conv_block, yh), x)
    conv_full = jnp.concatenate(conv_parts, axis=0)

    weights = jnp.concatenate(
        [
            w_sqkv.reshape(20, 576),
            w_sout.T,
            w_tqkv.reshape(20, 960),
            w_tout.T,
        ],
        axis=1,
    )
    keys, values = [stale_kv[:, :, :, k].reshape(FRAMES * COLUMNS, 192) for k in range(2)]
    kv = jnp.concatenate(
        [keys[:, :128], values[:, :128], keys[:, 128:], values[:, 128:]], axis=1
    )
    kv_other = from_shift(kv, "yh", 1)
    kv = [kv[:, :256], kv_other[:, :256], jnp.concatenate([kv[:, 256:], kv_other[:, 256:]], axis=1)]
    weights = pair_yh(weights, yh)
    weights = [weights[:, k * 256 : (k + 1) * 256] for k in range(8)]
    packed = jnp.concatenate(kv + weights, axis=0)
    packed = lax.all_gather(packed, ("z", "x"), axis=0, tiled=False)

    rows = jnp.concatenate([above, latent, below], axis=1).transpose(1, 0, 2, 3)
    rows = ring_gather(rows.reshape(3, FRAMES * COLUMNS, 320))
    half = shape((2, 128, 160), F32)
    keep, send = call(conv_kernel, (half, half), where, *rows, conv_full, smem=True, flops=3 * 10**9)
    mine, got = sum_over_frame(keep, send)

    def channels_of(vector):
        local = lax.dynamic_index_in_dim(vector.reshape(2, 8, 4, 20), z, 1, keepdims=False)
        return local.transpose(1, 0, 2).reshape(1, 160)

    embed = channels_of(lax.dynamic_index_in_dim(temb_table, step_index[0], 0, keepdims=False))
    hidden, stats = call(
        stats_kernel, (shape((128, 160), F32), shape((8, 128), F32)), mine, got, embed.astype(F32)
    )
    stats = lax.all_to_all(jnp.broadcast_to(stats, (8, 8, 128)), ("yh", "x"), 0, 0)
    activated = call(
        norm_kernel,
        shape((8, COLUMNS, 160), BF16),
        hidden,
        stats,
        channels_of(gn_gain),
        channels_of(gn_shift),
    )
    activated = lax.all_to_all(activated, "z", 0, 0)

    full = (FRAMES, COLUMNS, CHANNELS)
    part, fresh, own = call(
        spatial_kernel,
        (shape(full, BF16), shape((FRAMES, COLUMNS, 384), BF16), shape(full, BF16)),
        where,
        *gather_frame(activated),
        packed,
        smem=True,
        hbm=(5,),
        limit=56,
        scratch=[
            pltpu.VMEM((32, 120, 256), BF16),
            pltpu.VMEM((32, 192, 256), BF16),
            pltpu.SemaphoreType.DMA,
            pltpu.SemaphoreType.DMA,
        ],
        flops=10**9,
    )
    packed, part = lax.optimization_barrier((packed, part))
    second = packed[:, 312:]
    part, section = call(
        temporal_kernel,
        (shape(full, BF16), shape(full, BF16)),
        own,
        *sum_both(part),
        second,
        flops=10**9,
    )
    mine, got = sum_both(part)
    mixed = (section.astype(F32) + (mine.astype(F32) + got.astype(F32))).astype(BF16)
    return (
        mixed.reshape(FRAMES, 1, COLUMNS, CHANNELS),
        fresh.reshape(FRAMES, 1, COLUMNS, 2, 192),
    )


def solution(mesh):
    fine = Mesh(mesh.devices.reshape(2, 2, 2, 8, 4), ("yl", "c", "yh", "z", "x"))
    return jax.shard_map(
        shards,
        mesh=fine,
        in_specs=(
            P(None, PATCH, None, FRAME),
            P(None, PATCH, None, FRAME),
            P(None, FRAME, PATCH),
            P(),
            P(),
            P(),
            P(),
            P(PATCH, None, FRAME),
            P(None, PATCH, None, None, FRAME),
            P(FRAME, PATCH),
            P(PATCH, None, FRAME),
            P(FRAME, PATCH),
        ),
        out_specs=(P(None, PATCH, None, None), P(None, PATCH, None, None, FRAME)),
        check_vma=False,
    )
```

```python
import jax
import jax.numpy as jnp
from jax import lax
from jax.experimental import pallas as pl
from jax.experimental.pallas import tpu as pltpu
from jax.sharding import Mesh
from jax.sharding import PartitionSpec as P

CHANNELS = 1280
GROUPS = 32
GROUP_WIDTH = CHANNELS // GROUPS
HEAD_DIM = 64
FRAMES = 4
COLUMNS = 16
SIZES = {"yl": 2, "c": 2, "yh": 2, "z": 8, "x": 4}
FRAME = ("yl", "c")
PATCH = ("yh", "z", "x")
RING = (0, 1, 7, 2, 6, 3, 5, 4)
BF16 = jnp.bfloat16
F32 = jnp.float32
VMEM = pl.BlockSpec(memory_space=pltpu.VMEM)
SMEM = pl.BlockSpec(memory_space=pltpu.SMEM)
HBM = pl.BlockSpec(memory_space=pltpu.HBM)
NT = (((1,), (1,)), ((), ()))
TN = (((0,), (0,)), ((), ()))


def from_shift(value, axis, offset):
    size = SIZES[axis]
    return lax.ppermute(value, axis, [((i + offset) % size, i) for i in range(size)])


def ring_gather(block):
    ahead, behind = [block], [block]
    for _ in range(3):
        ahead.append(from_shift(ahead[-1], "z", 1))
        behind.append(from_shift(behind[-1], "z", -1))
    far = from_shift(ahead[-1], "z", 1)
    return [block, ahead[1], behind[1], ahead[2], behind[2], ahead[3], behind[3], far]


def pair_yh(block, yh):
    other = from_shift(block, "yh", 1)
    return jnp.concatenate(
        [jnp.where(yh == 0, block, other), jnp.where(yh == 0, other, block)], axis=0
    )


def gather_x(pair, x):
    parts = [pair] + [from_shift(pair, "x", k) for k in (1, 2, 3)]
    ordered = []
    for place in range(4):
        chosen = parts[place]
        for mine in (1, 2, 3):
            chosen = jnp.where(x == mine, parts[(place - mine) % 4], chosen)
        ordered.append(chosen)
    return ordered


def conv_kernel(where_ref, *refs):
    rows_refs, weight_ref, keep_ref, send_ref = refs[:8], refs[8], refs[9], refs[10]
    yl, c, z = where_ref[0], where_ref[1], where_ref[2]
    column = lax.broadcasted_iota(jnp.int32, (512, 1), 0) % COLUMNS
    sums = []
    for col_tap in range(3):
        total = None
        for row_tap in range(3):
            lhs = jnp.concatenate([r[row_tap] for r in rows_refs], axis=0)
            tap = 3 * row_tap + col_tap
            part = lax.dot_general(
                lhs,
                weight_ref[:, tap * 320 : (tap + 1) * 320],
                NT,
                preferred_element_type=F32,
            )
            total = part if total is None else total + part
        sums.append(total)
    left = jnp.where(column == 0, 0.0, pltpu.roll(sums[0], 1, 0))
    right = jnp.where(column == COLUMNS - 1, 0.0, pltpu.roll(sums[2], 511, 0))
    hidden = (sums[1] + left + right).reshape(8, FRAMES, COLUMNS, 160)
    for k, offset in enumerate(RING):
        start = pl.multiple_of((z + offset) % 8 * COLUMNS, COLUMNS)
        for frame in range(FRAMES):
            value = hidden[k, frame]
            place = yl ^ (frame // 2)

            @pl.when(c == frame % 2)
            def _():
                keep_ref[place, pl.ds(start, COLUMNS)] = value

            @pl.when(c != frame % 2)
            def _():
                send_ref[place, pl.ds(start, COLUMNS)] = value


def group_masks():
    lane = lax.broadcasted_iota(jnp.int32, (1, 160), 1)
    return [(lane // 80) * 2 + (lane % 40) // 20 == g for g in range(4)]


def stats_kernel(keep_ref, got_ref, embed_ref, hidden_ref, stats_ref):
    hidden = keep_ref[...] + got_ref[...] + embed_ref[...]
    hidden_ref[...] = hidden
    count = 128.0 * GROUP_WIDTH
    masks = group_masks()
    sums = jnp.sum(hidden, axis=0, keepdims=True)
    means = [jnp.sum(jnp.where(m, sums, 0.0), axis=1, keepdims=True) / count for m in masks]
    mean = sum(jnp.where(m, v, 0.0) for m, v in zip(masks, means))
    centred = hidden - mean
    squares = jnp.sum(centred * centred, axis=0, keepdims=True)
    lane = lax.broadcasted_iota(jnp.int32, (8, 128), 1)
    out = jnp.zeros((8, 128), F32)
    for g in range(4):
        spread = jnp.sum(jnp.where(masks[g], squares, 0.0), axis=1, keepdims=True)
        out = jnp.where(lane == g, means[g], out)
        out = jnp.where(lane == 4 + g, spread, out)
    stats_ref[...] = out


def norm_kernel(hidden_ref, stats_ref, gain_ref, shift_ref, out_ref):
    stats = stats_ref[...]
    masks = group_masks()
    local = 128.0 * GROUP_WIDTH
    mean_row = jnp.zeros((1, 160), F32)
    scale_row = jnp.zeros((1, 160), F32)
    for g in range(4):
        means = stats[:, 0:1, g : g + 1]
        mean = jnp.sum(means, axis=0, keepdims=True) / 8.0
        gap = means - mean
        spread = jnp.sum(stats[:, 0:1, 4 + g : 5 + g] + local * gap * gap, axis=0) / (8.0 * local)
        mean_row = jnp.where(masks[g], mean[0], mean_row)
        scale_row = jnp.where(masks[g], lax.rsqrt(spread + 1e-05), scale_row)
    normed = (hidden_ref[...] - mean_row) * scale_row
    value = normed * gain_ref[...] + shift_ref[...]
    out_ref[...] = jax.nn.silu(value).astype(BF16).reshape(8, COLUMNS, 160)


def softmax_parts(scores):
    top = jnp.max(scores, axis=-1, keepdims=True)
    expo = jnp.exp(scores - top)
    return expo.astype(BF16), jnp.sum(expo, axis=-1, keepdims=True)


def order_matrix():
    row = lax.broadcasted_iota(jnp.int32, (160, 160), 0)
    col = lax.broadcasted_iota(jnp.int32, (160, 160), 1)
    return (row // 40 * 20 + row % 20 + (row % 40) // 20 * 80 == col).astype(BF16)


def reorder_rows(turn, chunks):
    turned = []
    for rows in chunks:
        value = lax.dot_general(turn, rows, (((0,), (0,)), ((), ())), preferred_element_type=F32)
        turned.append(value.astype(BF16))
    return jnp.concatenate([t[80 * h : 80 * h + 80] for h in range(2) for t in turned], axis=0)


def chunk_of(w_ref, chunk, blocks):
    places = slice(4 * chunk, 4 * chunk + 4)
    parts = [w_ref[places, 40 * k : 40 * k + 40, :].reshape(160, 256) for k in blocks]
    return jnp.concatenate(parts, axis=1)


def spatial_kernel(where_ref, *refs):
    acts, packed_ref = refs[:4], refs[4]
    out_ref, fresh_ref, own_ref, w_scr, kv_scr, w_sem, kv_sem = refs[5:]
    w_copy = pltpu.make_async_copy(packed_ref.at[:, 192:312], w_scr, w_sem)
    kv_copy = pltpu.make_async_copy(packed_ref.at[:, :192], kv_scr, kv_sem)
    w_copy.start()
    kv_copy.start()
    yl, c, place = where_ref[0], where_ref[1], where_ref[2] * 4 + where_ref[4]
    frames = [(2 * yl + c) ^ rel for rel in range(FRAMES)]
    sources = [jnp.concatenate([a[chunk] for a in acts], axis=0) for chunk in range(8)]
    own = jnp.concatenate(sources, axis=1)
    for rel, frame in enumerate(frames):
        own_ref[frame] = own[rel * COLUMNS : (rel + 1) * COLUMNS]
    w_copy.wait()
    projected = None
    out_weights = []
    for chunk in range(8):
        rhs = chunk_of(w_scr, chunk, range(3))
        part = jnp.dot(sources[chunk], rhs[:, :576], preferred_element_type=F32)
        projected = part if projected is None else projected + part
        out_weights.append(rhs[:, 576:])
    projected = projected.astype(BF16)
    out_weights = jnp.concatenate(out_weights, axis=0)
    diagonal = lax.broadcasted_iota(jnp.int32, (48, 48), 0) == lax.broadcasted_iota(
        jnp.int32, (48, 48), 1
    )
    score_scale = HEAD_DIM ** (-0.5)
    head_of = lax.broadcasted_iota(jnp.int32, (COLUMNS, 192), 1) // HEAD_DIM
    key_row = lax.broadcasted_iota(jnp.int32, (512, 1), 0) // COLUMNS
    attended = []
    kv_copy.wait()
    for rel, frame in enumerate(frames):
        mine = projected[rel * COLUMNS : (rel + 1) * COLUMNS]
        fresh = mine[:, 192:]
        fresh_ref[frame] = fresh
        query = mine[:, :192]
        zero = jnp.zeros_like(query)
        queries = jnp.concatenate([jnp.where(head_of == h, query, zero) for h in range(3)], axis=0)
        start = pl.multiple_of(frame * COLUMNS, COLUMNS)
        low, high = [], []
        for half in range(2):
            rows = pl.ds(half * 64 + start, COLUMNS)
            low.append(kv_scr[:, rows, :].reshape(512, 256))
            rows = pl.ds(128 + start, COLUMNS)
            high.append(kv_scr[:, rows, half * 128 : half * 128 + 128].reshape(512, 128))
        scores = [lax.dot_general(fresh[:, :192], queries, NT, preferred_element_type=F32)]
        for a, b in zip(low, high):
            far = lax.dot_general(a[:, :128], queries[:, :128], NT, preferred_element_type=F32)
            scores.append(
                far
                + lax.dot_general(b[:, :64], queries[:, 128:], NT, preferred_element_type=F32)
            )
        scores = [s * score_scale for s in scores]
        scores[1] = jnp.where(key_row == place, -jnp.inf, scores[1])
        top = jnp.max(scores[0], axis=0, keepdims=True)
        for s in scores[1:]:
            top = jnp.maximum(top, jnp.max(s, axis=0, keepdims=True))
        expo = [jnp.exp(s - top) for s in scores]
        total = sum(jnp.sum(e, axis=0, keepdims=True) for e in expo)
        total = jnp.sum(jnp.where(diagonal, total, 0.0), axis=1, keepdims=True)
        expo = [e.astype(BF16) for e in expo]
        numerator = lax.dot_general(expo[0], fresh[:, 192:], TN, preferred_element_type=F32)
        for e, a, b in zip(expo[1:], low, high):
            values = jnp.concatenate([a[:, 128:], b[:, 64:]], axis=1)
            numerator = numerator + lax.dot_general(e, values, TN, preferred_element_type=F32)
        result = numerator / total
        rows = jnp.zeros((COLUMNS, 192), F32)
        for h in range(3):
            rows = jnp.where(head_of == h, result[h * COLUMNS : (h + 1) * COLUMNS], rows)
        attended.append(rows.astype(BF16))
    attended = jnp.concatenate(attended, axis=0)
    part = lax.dot_general(attended, out_weights, NT, preferred_element_type=F32)
    for rel, frame in enumerate(frames):
        out_ref[frame] = part[rel * COLUMNS : (rel + 1) * COLUMNS].astype(BF16)


def temporal_kernel(own_ref, mine_ref, got_ref, packed_ref, out_ref, section_ref):
    total = mine_ref[...].astype(F32) + got_ref[...].astype(F32)
    section = (own_ref[...].astype(F32) + total).astype(BF16).reshape(64, CHANNELS)
    sources = [section[:, chunk * 160 : (chunk + 1) * 160] for chunk in range(8)]
    temporal = None
    out_weights = []
    for chunk in range(8):
        rhs = chunk_of(packed_ref, chunk, range(5))
        part = jnp.dot(sources[chunk], rhs[:, :960], preferred_element_type=F32)
        temporal = part if temporal is None else temporal + part
        out_weights.append(rhs[:, 960:])
    temporal = temporal.astype(BF16)
    score_scale = HEAD_DIM ** (-0.5)
    row = lax.broadcasted_iota(jnp.int32, (64, 64), 0) % COLUMNS
    col = lax.broadcasted_iota(jnp.int32, (64, 64), 1) % COLUMNS
    outs = []
    for head in range(5):
        query, key, value = [
            temporal[:, k * 320 + head * 64 : k * 320 + (head + 1) * 64] for k in range(3)
        ]
        scores = lax.dot_general(query, key, NT, preferred_element_type=F32) * score_scale
        expo, total = softmax_parts(jnp.where(row == col, scores, -jnp.inf))
        outs.append(jnp.dot(expo, value, preferred_element_type=F32) / total)
    mixed = jnp.concatenate(outs, axis=1).astype(BF16)
    turn = order_matrix()
    turned = [jnp.dot(v, turn, preferred_element_type=F32).astype(BF16) for v in sources]
    turned = jnp.concatenate([t[:, 80 * h : 80 * h + 80] for h in range(2) for t in turned], axis=1)
    section_ref[...] = turned.reshape(FRAMES, COLUMNS, CHANNELS)
    part = lax.dot_general(
        mixed, reorder_rows(turn, out_weights), NT, preferred_element_type=F32
    )
    out_ref[...] = part.astype(BF16).reshape(FRAMES, COLUMNS, CHANNELS)


def call(kernel, out_shape, *args, scratch=(), flops=0, smem=False, hbm=(), limit=40):
    moved = sum(a.size * a.dtype.itemsize for a in args)
    return pl.pallas_call(
        kernel,
        out_shape=out_shape,
        in_specs=[
            SMEM if smem and i == 0 else HBM if i in hbm else VMEM for i in range(len(args))
        ],
        out_specs=jax.tree.map(lambda _: VMEM, out_shape),
        scratch_shapes=list(scratch),
        compiler_params=pltpu.CompilerParams(vmem_limit_bytes=limit * 1024 * 1024),
        cost_estimate=pl.CostEstimate(flops=flops, bytes_accessed=moved, transcendentals=0),
    )(*args)


def shape(dims, dtype):
    return jax.ShapeDtypeStruct(dims, dtype)


def swap(value, axis):
    return lax.ppermute(value, axis, [(0, 1), (1, 0)])


def sum_over_frame(keep, send):
    got = swap(send, "c")
    away = keep[1] + got[1]
    return keep[0] + got[0], swap(away, "yl")


def sum_both(part):
    mine = (part.astype(F32) + swap(part, "c").astype(F32)).astype(BF16)
    return mine, swap(mine, "yl")


def gather_frame(piece):
    other = swap(piece, "c")
    return [piece, other, swap(piece, "yl"), swap(other, "yl")]


def shards(
    latent,
    stale_latent,
    conv_weight,
    temb_table,
    step_index,
    gn_gain,
    gn_shift,
    w_sqkv,
    stale_kv,
    w_sout,
    w_tqkv,
    w_tout,
):
    yl, c, yh, z, x = (lax.axis_index(a) for a in ("yl", "c", "yh", "z", "x"))
    where = jnp.stack([yl, c, z, yh, x]).astype(jnp.int32)

    count = 64
    above = lax.ppermute(stale_latent, PATCH, [(i, i + 1) for i in range(count - 1)])
    below = lax.ppermute(stale_latent, PATCH, [(i + 1, i) for i in range(count - 1)])
    conv_block = jnp.transpose(conv_weight, (2, 0, 1)).reshape(20, 9 * 320)
    conv_parts = gather_x(pair_yh(conv_block, yh), x)
    conv_full = jnp.concatenate(conv_parts, axis=0)

    weights = jnp.concatenate(
        [
            w_sqkv.reshape(20, 576),
            w_sout.T,
            w_tqkv.reshape(20, 960),
            w_tout.T,
        ],
        axis=1,
    )
    keys, values = [stale_kv[:, :, :, k].reshape(FRAMES * COLUMNS, 192) for k in range(2)]
    kv = jnp.concatenate(
        [keys[:, :128], values[:, :128], keys[:, 128:], values[:, 128:]], axis=1
    )
    kv_other = from_shift(kv, "yh", 1)
    kv = [kv[:, :256], kv_other[:, :256], jnp.concatenate([kv[:, 256:], kv_other[:, 256:]], axis=1)]
    weights = pair_yh(weights, yh)
    weights = [weights[:, k * 256 : (k + 1) * 256] for k in range(8)]
    packed = jnp.concatenate(kv + weights, axis=0)
    packed = lax.all_gather(packed, ("z", "x"), axis=0, tiled=False)

    rows = jnp.concatenate([above, latent, below], axis=1).transpose(1, 0, 2, 3)
    rows = ring_gather(rows.reshape(3, FRAMES * COLUMNS, 320))
    half = shape((2, 128, 160), F32)
    keep, send = call(conv_kernel, (half, half), where, *rows, conv_full, smem=True, flops=3 * 10**9)
    mine, got = sum_over_frame(keep, send)

    def channels_of(vector):
        local = lax.dynamic_index_in_dim(vector.reshape(2, 8, 4, 20), z, 1, keepdims=False)
        return local.transpose(1, 0, 2).reshape(1, 160)

    embed = channels_of(lax.dynamic_index_in_dim(temb_table, step_index[0], 0, keepdims=False))
    hidden, stats = call(
        stats_kernel, (shape((128, 160), F32), shape((8, 128), F32)), mine, got, embed.astype(F32)
    )
    stats = lax.all_to_all(jnp.broadcast_to(stats, (8, 8, 128)), ("yh", "x"), 0, 0)
    activated = call(
        norm_kernel,
        shape((8, COLUMNS, 160), BF16),
        hidden,
        stats,
        channels_of(gn_gain),
        channels_of(gn_shift),
    )
    activated = lax.all_to_all(activated, "z", 0, 0)

    full = (FRAMES, COLUMNS, CHANNELS)
    part, fresh, own = call(
        spatial_kernel,
        (shape(full, BF16), shape((FRAMES, COLUMNS, 384), BF16), shape(full, BF16)),
        where,
        *gather_frame(activated),
        packed,
        smem=True,
        hbm=(5,),
        limit=56,
        scratch=[
            pltpu.VMEM((32, 120, 256), BF16),
            pltpu.VMEM((32, 192, 256), BF16),
            pltpu.SemaphoreType.DMA,
            pltpu.SemaphoreType.DMA,
        ],
        flops=10**9,
    )
    packed, part = lax.optimization_barrier((packed, part))
    second = packed[:, 312:]
    part, section = call(
        temporal_kernel,
        (shape(full, BF16), shape(full, BF16)),
        own,
        *sum_both(part),
        second,
        flops=10**9,
    )
    mine, got = sum_both(part)
    mixed = (section.astype(F32) + (mine.astype(F32) + got.astype(F32))).astype(BF16)
    return (
        mixed.reshape(FRAMES, 1, COLUMNS, CHANNELS),
        fresh.reshape(FRAMES, 1, COLUMNS, 2, 192),
    )


def solution(mesh):
    fine = Mesh(mesh.devices.reshape(2, 2, 2, 8, 4), ("yl", "c", "yh", "z", "x"))
    return jax.shard_map(
        shards,
        mesh=fine,
        in_specs=(
            P(None, PATCH, None, FRAME),
            P(None, PATCH, None, FRAME),
            P(None, FRAME, PATCH),
            P(),
            P(),
            P(),
            P(),
            P(PATCH, None, FRAME),
            P(None, PATCH, None, None, FRAME),
            P(FRAME, PATCH),
            P(PATCH, None, FRAME),
            P(FRAME, PATCH),
        ),
        out_specs=(P(None, PATCH, None, None), P(None, PATCH, None, None, FRAME)),
        check_vma=False,
    )
```
